256 devices in a mesh: tile: 256 (over x, y, z, core).
Axes of the slice: x: 4, y: 4, z: 8, core: 2. Of those that a mesh axis runs over, the one named last changes fastest.
Arguments:
- lam_parent: float32 [6, 50, 2048, 128], P(None, None, 'tile'), may hold values from -6 to 6
- lam_child: float32 [6, 50, 6144, 128], P(None, None, 'tile'), may hold values from -6 to 6
- kappa_parent: float32 [2048, 128], P('tile'), may hold values from 0.05 to 0.24
- kappa_child: float32 [6144, 128], P('tile'), may hold values from 0.05 to 0.24
- inv_parent: float32 [2048, 50, 50], P('tile'), may hold values from 0 to 1, as said below
- inv_child: float32 [6144, 50, 50], P('tile'), may hold values from 0 to 1, as said below
- bnd_child: int32 [8192], P('tile'), may hold values from 0 to 3071, as said below
- bnd_parent: int32 [8192], P('tile'), may hold values from 0 to 262143, as said below
- bnd_weight: float32 [8192], P('tile'), may hold values from 0.2 to 0.8
- upd_parent: int32 [8192], P('tile'), may hold values from 0 to 1023, as said below
- upd_child: int32 [8192], P('tile'), may hold values from 0 to 786431, as said below
- upd_weight: float32 [8192], P('tile'), may hold values from 0.2 to 0.8
Outputs:
- adj_parent: float32 [6, 50, 2048, 128], P(None, None, 'tile')
- adj_child: float32 [6, 50, 6144, 128], P(None, None, 'tile')
The draws below stay inside these ranges and needn't reach their ends.
Inputs may be any that keep to these rules, and one draw needn't show every extreme that they name: `bnd_child`: slot 0 is cell 0 and the last slot is the tile's last cell. The tile owning bnd_parent[s] differs from s // 32 by at most 4, and by exactly 4 for slot 1 of every device. `upd_parent`: slot 0 is cell 0 and the last slot is the tile's last cell. The tile owning upd_child[u] differs from u // 32 by at most 4, and by exactly 4 for slot 1 of every device. `inv_parent`: each row's matrix is dense and diagonally dominant with positive entries. `inv_child`: each row's matrix is dense and diagonally dominant with positive entries.
All inputs are finite; a program needn't handle non-finite values.
Results may differ from the reference program's by a relative error of at most 0.0001.
Values sent between devices are 32-bit elements; how exact they have to be, the bound alone decides.
No kernel may reach another device: no remote copies, remote signals or barrier semaphores. Data moves between devices by JAX's collectives and lax.ppermute only.
A program may use at most 64 MiB of HBM per device.

```python
import jax
import jax.numpy as jnp
from jax import lax

TR = 6
L = 50
W = 128
PR = 8
CR = 24
NB = 32
NU = 32
REACH = 4
NPR = 2048
NCR = 6144
N_TILE = 256


def inverse_table(key, rows, spread, low, high):
    key_diag, key_off = jax.random.split(key)
    diag = jax.random.uniform(key_diag, (rows, L), jnp.float32, low, high)
    level = jnp.arange(L, dtype=jnp.float32)
    gap = jnp.abs(level[:, None] - level[None, :])
    off = jax.random.uniform(key_off, (rows, L, L), jnp.float32) * jnp.exp(-gap / 6.0) * spread
    eye = jnp.eye(L, dtype=jnp.float32)
    return off * (1.0 - eye) + eye * diag[:, :, None]


def owner_list(key, per, count):
    n_dev = NPR // PR
    key_off, key_local = jax.random.split(key)
    slot_all = jnp.arange(n_dev * count, dtype=jnp.int32)
    device = slot_all // count
    slot = slot_all % count
    offset = jax.random.randint(key_off, (n_dev * count,), -REACH, REACH + 1)
    far = jnp.where(device + REACH < n_dev, REACH, -REACH)
    offset = jnp.where(slot == 1, far, offset)
    owner = jnp.clip(device + offset, 0, n_dev - 1)
    local = jax.random.randint(key_local, (n_dev * count,), 0, per)
    index = owner * per + local
    index = index.at[0].set(0).at[-1].set(n_dev * per - 1)
    return index.astype(jnp.int32)


def local_list(key, per, count):
    n_dev = NPR // PR
    local = jax.random.randint(key, (n_dev * count,), 0, per)
    local = local.at[0].set(0).at[-1].set(per - 1)
    return local.astype(jnp.int32)


def draw_inv_parent(key, part):
    key = jax.random.fold_in(key, 1)
    return inverse_table(key, NPR, 0.035, 0.5, 0.9)


def draw_inv_child(key, part):
    key = jax.random.fold_in(key, 2)
    return inverse_table(key, NCR, 0.035, 0.5, 0.9)


def draw_bnd_child(key, part):
    key = jax.random.fold_in(key, 3)
    return local_list(key, CR * W, NB)


def draw_bnd_parent(key, part):
    key = jax.random.fold_in(key, 4)
    return owner_list(key, PR * W, NB)


def draw_upd_parent(key, part):
    key = jax.random.fold_in(key, 5)
    return local_list(key, PR * W, NU)


def draw_upd_child(key, part):
    key = jax.random.fold_in(key, 6)
    return owner_list(key, CR * W, NU)


def block_scale(rng, extent, pieces, smallest, largest):
    level, own = 1.0, jax.random.fold_in(rng, 6)
    for axis_at, parts in pieces:
        draws = jnp.exp(jax.random.uniform(jax.random.fold_in(own, axis_at), (parts,), jnp.float32, smallest / len(pieces), largest / len(pieces)))
        level = level * jnp.repeat(draws, extent[axis_at] // parts).reshape([-1 if axis == axis_at else 1 for axis in range(len(extent))])
    return level


def scatter_about(stream_key, shape, width, reach, shards=(), kind=jnp.bfloat16):
    values = jax.random.normal(stream_key, shape, jnp.float32) * width
    if len(shards) > 0:
        values = block_scale(stream_key, shape, shards, -0.22, 0.18) * values
    return jnp.clip(values, min=-reach, max=reach).astype(kind)


def setup_inputs(seed: int = 0) -> dict:
    seeds = jax.random.split(jax.random.key(seed), 13)
    return {
        "lam_parent": scatter_about(seeds[0], (TR, L, NPR, W), 1.0, 6.0, ((2, 256),), jnp.float32),
        "lam_child": scatter_about(seeds[1], (TR, L, NCR, W), 1.0, 6.0, ((2, 256),), jnp.float32),
        "kappa_parent": jnp.clip(0.05 + 0.19 * jax.random.uniform(seeds[2], (NPR, W), jnp.float32) ** block_scale(seeds[2], (NPR, W), ((0, 256),), -0.2, 0.2), 0.05, 0.24),
        "kappa_child": jnp.clip(0.05 + 0.19 * jax.random.uniform(seeds[3], (NCR, W), jnp.float32) ** block_scale(seeds[3], (NCR, W), ((0, 256),), -0.2, 0.2), 0.05, 0.24),
        "inv_parent": draw_inv_parent(jax.random.fold_in(seeds[12], 71), 0),
        "inv_child": draw_inv_child(jax.random.fold_in(seeds[12], 71), 0),
        "bnd_child": draw_bnd_child(jax.random.fold_in(seeds[12], 71), 0),
        "bnd_parent": draw_bnd_parent(jax.random.fold_in(seeds[12], 71), 0),
        "bnd_weight": jnp.clip(0.2 + 0.6 * jax.random.uniform(seeds[8], (N_TILE * NB,), jnp.float32) ** block_scale(seeds[8], (N_TILE * NB,), ((0, 256),), -0.2, 0.2), 0.2, 0.8),
        "upd_parent": draw_upd_parent(jax.random.fold_in(seeds[12], 71), 0),
        "upd_child": draw_upd_child(jax.random.fold_in(seeds[12], 71), 0),
        "upd_weight": jnp.clip(0.2 + 0.6 * jax.random.uniform(seeds[11], (N_TILE * NU,), jnp.float32) ** block_scale(seeds[11], (N_TILE * NU,), ((0, 256),), -0.2, 0.2), 0.2, 0.8),
    }


def lap(v):
    padded = jnp.pad(v, ((0, 0), (0, 0), (1, 1), (1, 1)))
    return padded[:, :, 2:, 1:-1] + padded[:, :, :-2, 1:-1] + padded[:, :, 1:-1, 2:] + padded[:, :, 1:-1, :-2] - 4.0 * v

def vertical(matrix, field):
    return jnp.einsum('rlk,tkrc->tlrc', matrix, field, precision=lax.Precision.HIGHEST)

def reference(lam_parent, lam_child, kappa_parent, kappa_child, inv_parent, inv_child, bnd_child, bnd_parent, bnd_weight, upd_parent, upd_child, upd_weight):
    n_dev = NPR // PR
    chan = TR * L
    child_cell = jnp.arange(n_dev * NB, dtype=jnp.int32) // NB * (CR * W) + bnd_child.astype(jnp.int32)
    parent_cell = jnp.arange(n_dev * NU, dtype=jnp.int32) // NU * (PR * W) + upd_parent.astype(jnp.int32)

    def forward(start_parent, start_child):
        first = vertical(inv_parent, start_parent + kappa_parent * lap(start_parent))
        flat_parent = first.reshape(chan, -1)
        flat_child = start_child.reshape(chan, -1)
        flat_child = flat_child.at[:, child_cell].add(bnd_weight * (flat_parent[:, bnd_parent] - flat_child[:, child_cell]))
        state = flat_child.reshape(start_child.shape)
        for step in range(3):
            state = vertical(inv_child, state + kappa_child * lap(state))
        last_child = state.reshape(chan, -1)
        flat_parent = flat_parent.at[:, parent_cell].add(upd_weight * (last_child[:, upd_child] - flat_parent[:, parent_cell]))
        return (flat_parent.reshape(start_parent.shape), state)
    zeros_parent = jnp.zeros(lam_parent.shape, jnp.float32)
    zeros_child = jnp.zeros(lam_child.shape, jnp.float32)
    outputs, pullback = jax.vjp(forward, zeros_parent, zeros_child)
    adj_parent, adj_child = pullback((lam_parent, lam_child))
    return (adj_parent, adj_child)
```

```python
import functools

import jax
import jax.numpy as jnp
from jax import lax
from jax.experimental import pallas as pl
from jax.experimental.pallas import tpu as pltpu
from jax.sharding import PartitionSpec as P

F32, BF16 = jnp.float32, jnp.bfloat16
LEV, PAD, FULL = 50, 56, 64
MARK = 2 * PAD
UNITS = 11
VMEM_LIMIT = 40 * 1024 * 1024


def column(ref, k):
    return ref[:, k : k + 1]


def split(x):
    hi = x.astype(BF16)
    return hi, (x - hi.astype(F32)).astype(BF16)


def lanes(rows):
    return lax.broadcasted_iota(jnp.int32, (rows, 128), 1).astype(F32)


def hits(cells, row):
    return cells == lanes(cells.shape[0]) + float(row * 128)


def kept(cells, weights, row):
    return 1.0 - jnp.sum(jnp.where(hits(cells, row), weights, 0.0), axis=0, keepdims=True)


def padded_levels(x):
    return jnp.concatenate([x, jnp.zeros((PAD - LEV, 128), F32)], axis=0)


def picked(fields, marks):
    hi, lo = split(fields)
    return lax.dot_general(
        jnp.concatenate([marks, marks], axis=1),
        jnp.concatenate([hi, lo], axis=1),
        (((1,), (1,)), ((), ())),
        preferred_element_type=F32,
    )


def feed_row(sums, weights, targets):
    wide = jnp.concatenate([sums * weights, jnp.zeros((sums.shape[0], 128 - MARK), F32)], axis=1)
    return jnp.where(lanes(sums.shape[0]) == float(MARK), targets, wide)


def stacked_matrix(slab):
    turned = jnp.transpose(slab)[:FULL, :]
    wide = jnp.concatenate([turned, jnp.zeros((FULL, 128 - FULL), F32)], axis=1)
    hi = wide.astype(BF16).astype(F32)
    lo = wide - hi
    return jnp.concatenate(
        [hi + pltpu.roll(hi, FULL, 1), lo + pltpu.roll(lo, FULL, 1)], axis=1
    ).astype(BF16)


def matrices_kernel(inv_ref, out_ref, slab):
    slab[...] = jnp.zeros_like(slab)
    for r in range(inv_ref.shape[0]):
        slab[0:LEV, 0:LEV] = inv_ref[r]
        out_ref[r] = stacked_matrix(slab[...])


def matrices(inv):
    rows = inv.shape[0]
    return pl.pallas_call(
        matrices_kernel,
        out_shape=jax.ShapeDtypeStruct((rows, FULL, 256), BF16),
        scratch_shapes=[pltpu.VMEM((FULL, 128), F32)],
        compiler_params=pltpu.CompilerParams(vmem_limit_bytes=VMEM_LIMIT),
        name="matrices",
    )(inv)


def edge_slab(out_ref, at, inv, kappa):
    out_ref[(*at, 6)] = jnp.zeros((PAD, 128), F32)
    out_ref[(*at, 6, slice(0, LEV), slice(0, LEV))] = inv
    out_ref[(*at, 6, slice(LEV, LEV + 1), slice(None))] = kappa


def update_kernel(rows, small_ref, lam_ref, inv_ref, kappa_ref, feed_ref, sib_ref, cross_ref):
    cells, targets, weights = (column(small_ref, k) for k in (0, 1, 2))
    even = small_ref[0:1, 7:8] == 0.0
    last = rows - 1

    def level_rows(t, r):
        return padded_levels(lam_ref[pl.ds(t * LEV * rows + r, LEV, stride=rows), :])

    marks = [jnp.where(hits(cells, r), 1.0, 0.0).astype(BF16) for r in range(rows)]
    for g in range(3):
        total = jnp.zeros((cells.shape[0], MARK), F32)
        for r in range(rows):
            both = jnp.concatenate([level_rows(2 * g, r), level_rows(2 * g + 1, r)], axis=0)
            total = total + picked(both, marks[r])
        feed_ref[0, g] = feed_row(total, weights, targets)
    first_kept, last_kept = kept(cells, weights, 0), kept(cells, weights, last)
    for t in range(6):
        head = level_rows(t, 0) * first_kept
        tail = level_rows(t, last) * last_kept
        sib_ref[t] = jnp.where(even, tail, head)
        cross_ref[t] = jnp.where(even, head, tail)
    inv_head, inv_tail = inv_ref[0], inv_ref[last]
    k_head, k_tail = kappa_ref[0:1, :], kappa_ref[last : last + 1, :]
    edge_slab(sib_ref, (), jnp.where(even, inv_tail, inv_head), jnp.where(even, k_tail, k_head))
    edge_slab(cross_ref, (), jnp.where(even, inv_head, inv_tail), jnp.where(even, k_head, k_tail))


def updates(small, lam, inv, kappa):
    slots = small.shape[0]
    rows = kappa.shape[0]
    edge = jax.ShapeDtypeStruct((7, PAD, 128), F32)
    return pl.pallas_call(
        functools.partial(update_kernel, rows),
        out_shape=(jax.ShapeDtypeStruct((1, 3, slots, 128), F32), edge, edge),
        compiler_params=pltpu.CompilerParams(vmem_limit_bytes=VMEM_LIMIT),
        name="updates",
    )(small, lam, inv, kappa)


def edges_kernel(
    rows, halo, small_ref, first_ref, last_ref, inv_ref, kappa_ref, sib_ref, cross_ref
):
    even = small_ref[0:1, 7:8] == 0.0
    first, last = (ref.reshape(ref.shape[0] * 8, 128) for ref in (first_ref, last_ref))
    for j in range(halo):
        for t in range(6):
            head = padded_levels(first[pl.ds(t * LEV * 8 + j, LEV, stride=8), :])
            tail = padded_levels(last[pl.ds(t * LEV * 8 + 8 - halo + j, LEV, stride=8), :])
            sib_ref[j, t] = jnp.where(even, tail, head)
            cross_ref[j, t] = jnp.where(even, head, tail)
        b = rows - halo + j
        inv_head, inv_tail = inv_ref[j], inv_ref[b]
        k_head, k_tail = kappa_ref[j : j + 1, :], kappa_ref[b : b + 1, :]
        edge_slab(sib_ref, (j,), jnp.where(even, inv_tail, inv_head), jnp.where(even, k_tail, k_head))
        edge_slab(cross_ref, (j,), jnp.where(even, inv_head, inv_tail), jnp.where(even, k_head, k_tail))


def edges(small, lam, inv, kappa, halo):
    chan, rows, _ = lam.shape
    out = jax.ShapeDtypeStruct((halo, 7, PAD, 128), F32)
    whole = lambda x: pl.BlockSpec(x.shape, lambda i: (0,) * x.ndim)
    return pl.pallas_call(
        functools.partial(edges_kernel, rows, halo),
        grid=(1,),
        in_specs=[
            whole(small),
            pl.BlockSpec((chan, 8, 128), lambda i: (0, 0, 0)),
            pl.BlockSpec((chan, 8, 128), lambda i: (0, rows // 8 - 1, 0)),
            whole(inv),
            whole(kappa),
        ],
        out_specs=(whole(out), whole(out)),
        out_shape=(out, out),
        compiler_params=pltpu.CompilerParams(vmem_limit_bytes=VMEM_LIMIT),
        name="edges",
    )(small, lam, lam, inv, kappa)


def steps_kernel(rows, halo, steps, gather, *refs):
    (small_ref, lam_ref, feed_ref, sib_ref, cross_ref, sib_m, cross_m, mat_ref, kappa_ref), refs = (
        refs[:9],
        refs[9:],
    )
    if gather:
        out_ref, given_ref, *refs = refs
    else:
        out_ref, *refs = refs
    onehot, mats, coef, zbuf, *ybufs = refs
    grown = rows + 2 * halo
    even = small_ref[0:1, 7:8] == 0.0
    col = 3 if gather else 0
    cells, targets, weights = (column(small_ref, col + k) for k in range(3))

    @pl.when(pl.program_id(0) == 0)
    def prepare():
        mats[halo : halo + rows] = mat_ref[...]
        zero = jnp.zeros((FULL - PAD, 128), F32)
        kap = [None] * grown
        for j in range(halo):
            low = jnp.where(even, cross_m[j, 0], sib_m[j, 0])
            high = jnp.where(even, sib_m[j, 0], cross_m[j, 0])
            for q, slab in ((j, low), (halo + rows + j, high)):
                mats[q] = stacked_matrix(jnp.concatenate([slab, zero], axis=0))
                kap[q] = slab[LEV : LEV + 1, :]
        for r in range(rows):
            kap[halo + r] = kappa_ref[r : r + 1, :]
        lane = lax.broadcasted_iota(jnp.int32, (1, 128), 1)
        for q in range(grown):
            k = kap[q]
            coef[0, q : q + 1, :] = k
            coef[1, q : q + 1, :] = jnp.where(lane == 0, 0.0, pltpu.roll(k, 1, 1))
            coef[2, q : q + 1, :] = jnp.where(lane == 127, 0.0, pltpu.roll(k, 127, 1))
            coef[3, q : q + 1, :] = 1.0 - 4.0 * k
        for r in range(rows):
            coef[4, r : r + 1, :] = kept(cells, weights, r)
        slots = feed_ref.shape[0] * feed_ref.shape[2]
        names = feed_ref[:, 0].reshape(slots, 128)[:, MARK : MARK + 1]
        base = (small_ref[0:1, 6:7] * float(rows) - float(halo)) * 128.0
        names = names - base
        for q in range(grown):
            onehot[q // 2, :, (q % 2) * 128 : (q % 2) * 128 + 128] = jnp.where(
                hits(names, q), 1.0, 0.0
            ).astype(BF16)

    slots = feed_ref.shape[0] * feed_ref.shape[2]
    feeds = jnp.transpose(feed_ref[:, 0].reshape(slots, 128))[:MARK, :]
    feed_hi = feeds.astype(BF16).astype(F32)
    feeds = jnp.concatenate([feed_hi, feeds - feed_hi], axis=0).astype(BF16)
    tail_rows = jnp.zeros((FULL - PAD, 256), F32)

    def store(q, z):
        hi, lo = split(jnp.concatenate([z, tail_rows], axis=0))
        zbuf[q, 0:FULL] = hi
        zbuf[q, FULL : 2 * FULL] = lo

    arrived = {}

    def start(q):
        if q % 2 == 0:
            both = jnp.dot(feeds, onehot[q // 2], preferred_element_type=F32)
            arrived[q // 2] = both[:MARK] + both[MARK:]
        here = arrived[q // 2][:, (q % 2) * 128 : (q % 2) * 128 + 128]
        parts = []
        r = q - halo
        for t in range(2):
            if 0 <= r < rows:
                x = padded_levels(lam_ref[pl.ds(t * LEV * rows + r, LEV, stride=rows), :])
                if not gather:
                    x = x * coef[4, r : r + 1, :]
            else:
                low = q < halo
                j = q if low else q - halo - rows
                a, b = (cross_ref, sib_ref) if low else (sib_ref, cross_ref)
                x = jnp.where(even, a[j, t], b[j, t])
            parts.append(x + here[t * PAD : (t + 1) * PAD])
        store(q, jnp.concatenate(parts, axis=1))

    def lift(k, q):
        z = zbuf[q]
        y = jnp.dot(mats[q], jnp.concatenate([z, z], axis=0), preferred_element_type=F32)
        ybufs[k][q] = y[:PAD]

    def spread(k, q):
        parts = []
        for t in range(2):
            s = slice(t * 128, t * 128 + 128)
            y = ybufs[k][q, :, s]
            z = y * coef[3, q : q + 1, :]
            z = z + pltpu.roll(y, 1, 1) * coef[1, q : q + 1, :]
            z = z + pltpu.roll(y, 127, 1) * coef[2, q : q + 1, :]
            z = z + ybufs[k][q - 1, :, s] * coef[0, q - 1 : q, :]
            z = z + ybufs[k][q + 1, :, s] * coef[0, q + 1 : q + 2, :]
            parts.append(z)
        if k < steps - 1:
            store(q, jnp.concatenate(parts, axis=1))
            return
        r = q - halo
        for t in range(2):
            z = parts[t]
            if gather:
                z = z * coef[4, r : r + 1, :]
            out_ref[pl.ds(t * LEV * rows + r, LEV, stride=rows), :] = z[:LEV]
        if gather:
            marks = jnp.where(hits(cells, r), 1.0, 0.0).astype(BF16)
            totals.append(picked(jnp.concatenate(parts, axis=0), marks))
            if len(totals) == 2:
                totals[:] = [totals[0] + totals[1]]

    totals = []
    plan = []
    for q in range(grown):
        plan.append((q, 0, start, (q,)))
        for k in range(steps):
            if k <= q < grown - k:
                plan.append((q + 1 + 3 * k, 1 + 2 * k, lift, (k, q)))
            if k + 1 <= q < grown - k - 1:
                plan.append((q + 3 + 3 * k, 2 + 2 * k, spread, (k, q)))
    for _, _, act, args in sorted(plan, key=lambda p: p[:2]):
        act(*args)
    if gather:
        given_ref[0, 0] = feed_row(totals[0], weights, targets)


def run_steps(small, lam, feeds, sib, cross, mats, kappa, halo, steps, gather):
    rows = kappa.shape[0]
    grown = rows + 2 * halo
    units, _, slots, _ = feeds.shape
    whole = lambda x: pl.BlockSpec(x.shape, lambda g: (0,) * x.ndim)
    field = pl.BlockSpec((2 * LEV * rows, 128), lambda g: (g, 0))
    edge = pl.BlockSpec((halo, 2, PAD, 128), lambda g: (0, g, 0, 0))
    slab = pl.BlockSpec((halo, 1, PAD, 128), lambda g: (0, 6, 0, 0))
    out_shape = [jax.ShapeDtypeStruct(lam.shape, F32)]
    out_specs = [field]
    if gather:
        out_shape.append(jax.ShapeDtypeStruct((1, 3, small.shape[0], 128), F32))
        out_specs.append(pl.BlockSpec((1, 1, small.shape[0], 128), lambda g: (0, g, 0, 0)))
    return pl.pallas_call(
        functools.partial(steps_kernel, rows, halo, steps, gather),
        grid=(3,),
        in_specs=[
            whole(small),
            field,
            pl.BlockSpec((units, 1, slots, 128), lambda g: (0, g, 0, 0)),
            edge,
            edge,
            slab,
            slab,
            whole(mats),
            whole(kappa),
        ],
        out_specs=out_specs,
        out_shape=out_shape,
        scratch_shapes=[
            pltpu.VMEM((grown // 2, units * slots, 256), BF16),
            pltpu.VMEM((grown, FULL, 256), BF16),
            pltpu.VMEM((5, (grown + 7) // 8 * 8, 128), F32),
            pltpu.VMEM((grown, 2 * FULL, 256), BF16),
        ]
        + [pltpu.VMEM((grown, PAD, 256), F32) for _ in range(steps)],
        compiler_params=pltpu.CompilerParams(vmem_limit_bytes=VMEM_LIMIT),
        name="child" if gather else "parent",
    )(small, lam, feeds, sib, cross, sib, cross, mats, kappa)


def sibling(x):
    count = lax.axis_size("tile")
    return lax.ppermute(x, "tile", [(i, i ^ 1) for i in range(count)])


def across(x):
    count = lax.axis_size("tile")
    low = range(1, count - 1, 2)
    return lax.ppermute(x, "tile", [(i, i + 1) for i in low] + [(i + 1, i) for i in low])


def all_near(own):
    join = lambda *xs: jnp.concatenate(xs, axis=0)
    chip = join(own, sibling(own))
    one = across(chip)
    other = sibling(one)
    two = across(other)
    second = sibling(two)
    three = across(second[:1])
    return join(chip, one, other, two, second, three)


def per_device(
    lam_parent,
    lam_child,
    kappa_parent,
    kappa_child,
    inv_parent,
    inv_child,
    bnd_child,
    bnd_parent,
    bnd_weight,
    upd_parent,
    upd_child,
    upd_weight,
):
    me = lax.axis_index("tile")
    slots = bnd_child.shape[0]
    columns = [upd_parent, upd_child, upd_weight, bnd_child, bnd_parent, bnd_weight]
    columns = [c.astype(F32) for c in columns]
    columns += [jnp.full((slots,), v.astype(F32)) for v in (me, me % 2)]
    small = jnp.pad(jnp.stack(columns, axis=1), ((0, 0), (0, 128 - len(columns))))
    flat_parent = lam_parent.reshape(-1, 128)
    flat_child = lam_child.reshape(-1, 128)
    feed, mu_sib, mu_cross = updates(small, flat_parent, inv_parent, kappa_parent)
    feeds = all_near(feed)
    child_edges = edges(
        small, lam_child.reshape(-1, *lam_child.shape[2:]), inv_child, kappa_child, 3
    )
    child_sib, child_cross = sibling(child_edges[0]), across(child_edges[1])
    mu_sib, mu_cross = sibling(mu_sib[None]), across(mu_cross[None])
    adj_child, given = run_steps(
        small, flat_child, feeds, child_sib, child_cross, matrices(inv_child), kappa_child, 3, 3, True
    )
    (adj_parent,) = run_steps(
        small, flat_parent, all_near(given), mu_sib, mu_cross, matrices(inv_parent), kappa_parent, 1, 1, False
    )
    return adj_parent.reshape(lam_parent.shape), adj_child.reshape(lam_child.shape)


def solution(mesh):
    field, plane, cube, line = P(None, None, "tile", None), P("tile", None), P("tile", None, None), P("tile")
    in_specs = (field, field, plane, plane, cube, cube) + (line,) * 6
    return jax.shard_map(
        per_device, mesh=mesh, in_specs=in_specs, out_specs=(field, field), check_vma=False
    )
```

```python
import functools

import jax
import jax.numpy as jnp
from jax import lax
from jax.experimental import pallas as pl
from jax.experimental.pallas import tpu as pltpu
from jax.sharding import PartitionSpec as P

F32, BF16 = jnp.float32, jnp.bfloat16
LEV, PAD, FULL = 50, 56, 64
MARK = 2 * PAD
VMEM_LIMIT = 40 * 1024 * 1024


def columns(rows, lists):
    rows[...] = jnp.zeros_like(rows)
    for k, ref in enumerate(lists):
        rows[k : k + 1, 0 : ref.shape[1]] = ref[...].astype(F32)
    turned = jnp.transpose(rows[...])[: lists[0].shape[1]]
    return [turned[:, k : k + 1] for k in range(len(lists))]


def on_even():
    return lax.rem(lax.axis_index("tile"), 2) == 0


def split(x):
    hi = x.astype(BF16)
    return hi, (x - hi.astype(F32)).astype(BF16)


def lanes(rows):
    return lax.broadcasted_iota(jnp.int32, (rows, 128), 1).astype(F32)


def hits(cells, row):
    return cells == lanes(cells.shape[0]) + jnp.asarray(row * 128, F32)


def kept(cells, weights, row):
    return 1.0 - jnp.sum(jnp.where(hits(cells, row), weights, 0.0), axis=0, keepdims=True)


def padded_levels(x):
    return jnp.concatenate([x, jnp.zeros((PAD - LEV, 128), F32)], axis=0)


def picked(fields, marks):
    hi, lo = split(fields)
    return lax.dot_general(
        jnp.concatenate([marks, marks], axis=1),
        jnp.concatenate([hi, lo], axis=1),
        (((1,), (1,)), ((), ())),
        preferred_element_type=F32,
    )


def feed_row(sums, weights, targets):
    wide = jnp.concatenate([sums * weights, jnp.zeros((sums.shape[0], 128 - MARK), F32)], axis=1)
    return jnp.where(lanes(sums.shape[0]) == float(MARK), targets, wide)


def stacked_matrix(slab):
    turned = jnp.transpose(slab)[:FULL, :]
    wide = jnp.concatenate([turned, jnp.zeros((FULL, 128 - FULL), F32)], axis=1)
    hi = wide.astype(BF16).astype(F32)
    lo = wide - hi
    return jnp.concatenate(
        [hi + pltpu.roll(hi, FULL, 1), lo + pltpu.roll(lo, FULL, 1)], axis=1
    ).astype(BF16)


def matrices_kernel(rows, inv_ref, out_ref, slab):
    slab[...] = jnp.zeros_like(slab)
    for r in range(rows):
        slab[0:LEV, 0:LEV] = inv_ref[pl.ds(r, LEV, stride=rows), :]
        out_ref[r] = stacked_matrix(slab[...])


def matrices(inv, rows):
    return pl.pallas_call(
        functools.partial(matrices_kernel, rows),
        out_shape=jax.ShapeDtypeStruct((rows, FULL, 256), BF16),
        scratch_shapes=[pltpu.VMEM((FULL, 128), F32)],
        compiler_params=pltpu.CompilerParams(vmem_limit_bytes=VMEM_LIMIT),
        name="matrices",
    )(inv)


def pack_row(ref, j, field, inv_ref, kappa_ref, row, rows, slab):
    slab[0:LEV, 0:LEV] = inv_ref[pl.ds(row, LEV, stride=rows), :]
    slab[FULL : FULL + 32] = slab[0:32] + pltpu.roll(slab[LEV // 2 : LEV // 2 + 32], 64, 1)
    for t in range(6):
        top = (6 * j + t) * PAD
        pad = top + LEV
        ref[top:pad] = field(t)
        if t < 5:
            ref[pad : pad + 5] = slab[FULL + 5 * t : FULL + 5 * t + 5]
            ref[pad + 5 : pad + 6] = jnp.zeros((1, 128), F32)
        else:
            ref[pad : pad + 1] = kappa_ref[pl.ds(row, 1), :]
            ref[pad + 1 : pad + 6] = jnp.zeros((5, 128), F32)


def unpacked_matrix(slabs, slab):
    half = LEV // 2
    slab[...] = jnp.zeros_like(slab)
    for t in range(5):
        slab[FULL + 5 * t : FULL + 5 * t + 5] = slabs(t)[LEV : LEV + 5]
    both = slab[FULL : FULL + 32]
    low = lax.broadcasted_iota(jnp.int32, both.shape, 1) < LEV
    slab[0:half] = jnp.where(low, both, 0.0)[:half]
    slab[half:LEV] = jnp.where(low, pltpu.roll(both, 64, 1), 0.0)[:half]
    return slab[0:FULL]


def prepare_kernel(halo, *refs):
    sources, refs = refs[:9], refs[9:]
    feed_ref, sib_ref, cross_ref, *refs = refs
    local, (names, slab, arrived) = refs[:9], refs[9:]
    copies = [
        pltpu.make_async_copy(source, target, arrived.at[k])
        for k, (source, target) in enumerate(zip(sources, local))
    ]
    for copy in copies:
        copy.start()
    lists, (lam_ref, inv_ref, kappa_ref) = local[:3], local[3:6]
    rows = kappa_ref.shape[0]
    for copy in copies[:4]:
        copy.wait()
    cells, targets, weights = columns(names, lists)

    def level_rows(t, r):
        return lam_ref[pl.ds(t * LEV * rows + r, LEV, stride=rows), :]

    marks = [jnp.where(hits(cells, r), 1.0, 0.0).astype(BF16) for r in range(rows)]
    for g in range(3):
        total = jnp.zeros((cells.shape[0], MARK), F32)
        for r in range(rows):
            both = [padded_levels(level_rows(2 * g + t, r)) for t in range(2)]
            total = total + picked(jnp.concatenate(both, axis=0), marks[r])
        row = feed_row(total, weights, targets)
        feed_ref[0, g] = row
        slots = row.shape[0]
        at = (halo + 1) * 6 * PAD + g * slots
        cross_ref[at : at + slots] = row
    slab[...] = jnp.zeros_like(slab)
    even = on_even()
    for copy in copies[4:]:
        copy.wait()
    for ref, head in ((sib_ref, ~even), (cross_ref, even)):
        r = jnp.where(head, 0, rows - 1)
        left = kept(cells, weights, r)
        field = lambda t: level_rows(t, r) * left
        pack_row(ref, halo, field, inv_ref, kappa_ref, r, rows, slab)
        child_ref, child_inv, child_kappa = local[6:9]
        crows = child_kappa.shape[0]
        for j in range(halo):
            r = jnp.where(head, j, crows - halo + j)
            field = lambda t: child_ref[pl.ds(t * LEV * crows + r, LEV, stride=crows), :]
            pack_row(ref, j, field, child_inv, child_kappa, r, crows, slab)


def prepare(lists, lam, inv, kappa, child, child_inv, child_kappa, halo):
    slots = lists[0].shape[1]
    edge = (halo + 1) * 6 * PAD
    operands = (*lists, lam, inv, kappa, child, child_inv, child_kappa)
    return pl.pallas_call(
        functools.partial(prepare_kernel, halo),
        in_specs=[pl.BlockSpec(memory_space=pltpu.HBM)] * len(operands),
        out_shape=(
            jax.ShapeDtypeStruct((1, 3, slots, 128), F32),
            jax.ShapeDtypeStruct((edge, 128), F32),
            jax.ShapeDtypeStruct((edge + 6 * slots, 128), F32),
        ),
        scratch_shapes=[pltpu.VMEM(x.shape, x.dtype) for x in operands]
        + [
            pltpu.VMEM((8, 128), F32),
            pltpu.VMEM((2 * FULL, 128), F32),
            pltpu.SemaphoreType.DMA((len(operands),)),
        ],
        compiler_params=pltpu.CompilerParams(vmem_limit_bytes=62 * 1024 * 1024),
        name="prepare",
    )(*operands)


def steps_kernel(rows, halo, steps, gather, places, *refs):
    lists, refs = refs[:3], refs[3:]
    feed_refs, refs = refs[: len(places)], refs[len(places) :]
    (lam_ref, sib_ref, cross_ref, mat_ref, kappa_ref), refs = refs[:5], refs[5:]
    if gather:
        out_ref, given_ref, *refs = refs
    else:
        out_ref, *refs = refs
    onehot, mats, coef, zbuf, names, slab, *ybufs = refs
    grown = rows + 2 * halo
    group = pl.program_id(0)
    even = on_even()
    cells, targets, weights = columns(names, lists)
    slots = targets.shape[0]
    units = sum(count for _, count in places)
    feeds = jnp.concatenate(
        [
            ref[pl.ds(pl.multiple_of(start + (3 * u + group) * slots, 8), slots), :]
            for ref, (start, count) in zip(feed_refs, places)
            for u in range(count)
        ],
        axis=0,
    )
    first_edge = 0 if gather else sib_ref.shape[0] // (6 * PAD) - 1

    def edge_row(ref, j, t):
        at = ((first_edge + j) * 6 + t) * PAD
        return ref[pl.ds(at if isinstance(at, int) else pl.multiple_of(at, 8), PAD), :]

    def low_row(j, t):
        return jnp.where(even, edge_row(cross_ref, j, t), edge_row(sib_ref, j, t))

    def high_row(j, t):
        return jnp.where(even, edge_row(sib_ref, j, t), edge_row(cross_ref, j, t))

    @pl.when(pl.program_id(0) == 0)
    def prepare():
        mats[halo : halo + rows] = mat_ref[...]
        kap = [None] * grown
        for j in range(halo):
            for q, row in ((j, low_row), (halo + rows + j, high_row)):
                slabs = functools.partial(row, j)
                mats[q] = stacked_matrix(unpacked_matrix(slabs, slab))
                kap[q] = slabs(5)[LEV : LEV + 1, :]
        for r in range(rows):
            kap[halo + r] = kappa_ref[r : r + 1, :]
        lane = lax.broadcasted_iota(jnp.int32, (1, 128), 1)
        for q in range(grown):
            k = kap[q]
            coef[0, q : q + 1, :] = k
            coef[1, q : q + 1, :] = jnp.where(lane == 0, 0.0, pltpu.roll(k, 1, 1))
            coef[2, q : q + 1, :] = jnp.where(lane == 127, 0.0, pltpu.roll(k, 127, 1))
            coef[3, q : q + 1, :] = 1.0 - 4.0 * k
        for r in range(rows):
            coef[4, r : r + 1, :] = kept(cells, weights, r)
        base = (lax.axis_index("tile") * rows - halo) * 128
        reached = feeds[:, MARK : MARK + 1] - base.astype(F32)
        for q in range(grown):
            onehot[q // 2, :, (q % 2) * 128 : (q % 2) * 128 + 128] = jnp.where(
                hits(reached, q), 1.0, 0.0
            ).astype(BF16)

    feeds = jnp.transpose(feeds)[:MARK, :]
    feed_hi = feeds.astype(BF16).astype(F32)
    feeds = jnp.concatenate([feed_hi, feeds - feed_hi], axis=0).astype(BF16)
    tail_rows = jnp.zeros((FULL - PAD, 256), F32)

    def store(q, z):
        hi, lo = split(jnp.concatenate([z, tail_rows], axis=0))
        zbuf[q, 0:FULL] = hi
        zbuf[q, FULL : 2 * FULL] = lo

    arrived = {}

    def start(q):
        if q % 2 == 0:
            both = jnp.dot(feeds, onehot[q // 2], preferred_element_type=F32)
            arrived[q // 2] = both[:MARK] + both[MARK:]
        here = arrived[q // 2][:, (q % 2) * 128 : (q % 2) * 128 + 128]
        parts = []
        r = q - halo
        for t in range(2):
            if 0 <= r < rows:
                x = padded_levels(lam_ref[pl.ds(t * LEV * rows + r, LEV, stride=rows), :])
                if not gather:
                    x = x * coef[4, r : r + 1, :]
            else:
                at = 2 * group + t
                x = low_row(q, at) if q < halo else high_row(q - halo - rows, at)
            parts.append(x + here[t * PAD : (t + 1) * PAD])
        store(q, jnp.concatenate(parts, axis=1))

    def lift(k, q):
        z = zbuf[q]
        y = jnp.dot(mats[q], jnp.concatenate([z, z], axis=0), preferred_element_type=F32)
        ybufs[k][q] = y[:PAD]

    def spread(k, q):
        parts = []
        for t in range(2):
            s = slice(t * 128, t * 128 + 128)
            y = ybufs[k][q, :, s]
            z = y * coef[3, q : q + 1, :]
            z = z + pltpu.roll(y, 1, 1) * coef[1, q : q + 1, :]
            z = z + pltpu.roll(y, 127, 1) * coef[2, q : q + 1, :]
            z = z + ybufs[k][q - 1, :, s] * coef[0, q - 1 : q, :]
            z = z + ybufs[k][q + 1, :, s] * coef[0, q + 1 : q + 2, :]
            parts.append(z)
        if k < steps - 1:
            store(q, jnp.concatenate(parts, axis=1))
            return
        r = q - halo
        for t in range(2):
            z = parts[t]
            if gather:
                z = z * coef[4, r : r + 1, :]
            out_ref[pl.ds(t * LEV * rows + r, LEV, stride=rows), :] = z[:LEV]
        if gather:
            marks = jnp.where(hits(cells, r), 1.0, 0.0).astype(BF16)
            totals.append(picked(jnp.concatenate(parts, axis=0), marks))
            if len(totals) == 2:
                totals[:] = [totals[0] + totals[1]]

    totals = []
    plan = []
    for q in range(grown):
        plan.append((q, 0, start, (q,)))
        for k in range(steps):
            if k <= q < grown - k:
                plan.append((q + 1 + 3 * k, 1 + 2 * k, lift, (k, q)))
            if k + 1 <= q < grown - k - 1:
                plan.append((q + 3 + 3 * k, 2 + 2 * k, spread, (k, q)))
    for _, _, act, args in sorted(plan, key=lambda p: p[:2]):
        act(*args)
    if gather:
        given_ref[0, 0] = feed_row(totals[0], weights, targets)


def run_steps(lists, feeds, lam, sib, cross, mats, kappa, halo, steps, gather):
    rows = kappa.shape[0]
    grown = rows + 2 * halo
    slots = lists[0].shape[1]
    places = tuple((start, count) for _, start, count in feeds)
    feeds = [x for x, _, _ in feeds]
    units = sum(count for _, count in places)
    whole = lambda x: pl.BlockSpec(x.shape, lambda g: (0,) * x.ndim)
    field = pl.BlockSpec((2 * LEV * rows, 128), lambda g: (g, 0))
    out_shape = [jax.ShapeDtypeStruct(lam.shape, F32)]
    out_specs = [field]
    if gather:
        out_shape.append(jax.ShapeDtypeStruct((1, 3, slots, 128), F32))
        out_specs.append(pl.BlockSpec((1, 1, slots, 128), lambda g: (0, g, 0, 0)))
    return pl.pallas_call(
        functools.partial(steps_kernel, rows, halo, steps, gather, places),
        grid=(3,),
        in_specs=[whole(x) for x in (*lists, *feeds)]
        + [field, whole(sib), whole(cross), whole(mats), whole(kappa)],
        out_specs=out_specs,
        out_shape=out_shape,
        scratch_shapes=[
            pltpu.VMEM((grown // 2, units * slots, 256), BF16),
            pltpu.VMEM((grown, FULL, 256), BF16),
            pltpu.VMEM((5, (grown + 7) // 8 * 8, 128), F32),
            pltpu.VMEM((grown, 2 * FULL, 256), BF16),
            pltpu.VMEM((8, 128), F32),
            pltpu.VMEM((2 * FULL, 128), F32),
        ]
        + [pltpu.VMEM((grown, PAD, 256), F32) for _ in range(steps)],
        compiler_params=pltpu.CompilerParams(vmem_limit_bytes=VMEM_LIMIT),
        name="child" if gather else "parent",
    )(*lists, *feeds, lam, sib, cross, mats, kappa)


def exchange(x, pairs):
    return lax.ppermute(x, "tile", [p for a, b in pairs for p in ((a, b), (b, a))])


def sibling(x):
    return exchange(x, [(i, i + 1) for i in range(0, lax.axis_size("tile"), 2)])


def beyond(x, distance):
    count = lax.axis_size("tile")
    return exchange(x, [(i, i + distance) for i in range(1, count - distance, 2)])


def rows_of(x):
    return x.reshape(-1, 128)


def per_device(
    lam_parent,
    lam_child,
    kappa_parent,
    kappa_child,
    inv_parent,
    inv_child,
    bnd_child,
    bnd_parent,
    bnd_weight,
    upd_parent,
    upd_child,
    upd_weight,
):
    upd = [x.reshape(1, -1) for x in (upd_parent, upd_child, upd_weight)]
    bnd = [x.reshape(1, -1) for x in (bnd_child, bnd_parent, bnd_weight)]
    flat_parent = lam_parent.reshape(-1, 128)
    flat_child = lam_child.reshape(-1, 128)
    inv_parent, inv_child = (
        jnp.transpose(x, (1, 0, 2)).reshape(-1, x.shape[2]) for x in (inv_parent, inv_child)
    )
    feed, to_sib, to_cross = prepare(
        upd, flat_parent, inv_parent, kappa_parent, flat_child, inv_child, kappa_child, 3
    )
    slots = bnd_child.shape[0]
    unit = 3 * slots

    beside = sibling(feed)
    last = to_cross.shape[0] - unit
    to_cross = lax.dynamic_update_slice(to_cross, rows_of(beside), (last, 0))
    far = beyond(feed, 5)
    chip = jnp.concatenate([feed, beside], axis=0)
    two = beyond(chip, 3)
    cross = beyond(to_cross, 1)
    fetched = jnp.concatenate([cross[last - unit :], rows_of(two), rows_of(far)], axis=0)
    feeds = [(rows_of(chip), 0, 2), (fetched, 0, 5), (sibling(fetched), 0, 4)]
    sib = sibling(to_sib)
    adj_child, given = run_steps(
        bnd, feeds, flat_child, sib, cross, matrices(inv_child, kappa_child.shape[0]), kappa_child, 3, 3, True
    )
    far = beyond(given, 5)
    chip = jnp.concatenate([given, sibling(given)], axis=0)
    fetched = jnp.concatenate([beyond(chip, 1), beyond(chip, 3), far], axis=0)
    feeds = [(rows_of(chip), 0, 2), (rows_of(fetched), 0, 5), (rows_of(sibling(fetched)), 0, 4)]
    (adj_parent,) = run_steps(
        upd, feeds, flat_parent, sib, cross, matrices(inv_parent, kappa_parent.shape[0]), kappa_parent, 1, 1, False
    )
    return adj_parent.reshape(lam_parent.shape), adj_child.reshape(lam_child.shape)


def solution(mesh):
    field, plane = P(None, None, "tile", None), P("tile", None)
    cube, line = P("tile", None, None), P("tile")
    in_specs = (field, field, plane, plane, cube, cube) + (line,) * 6
    return jax.shard_map(
        per_device, mesh=mesh, in_specs=in_specs, out_specs=(field, field), check_vma=False
    )
```

```python
import functools

import jax
import jax.numpy as jnp
from jax import lax
from jax.experimental import pallas as pl
from jax.experimental.pallas import tpu as pltpu
from jax.sharding import PartitionSpec as P

F32, BF16 = jnp.float32, jnp.bfloat16
LEV, PAD, FULL = 50, 56, 64
FEW = 128
MARK = 2 * PAD
VMEM_LIMIT = 40 * 1024 * 1024


def columns(rows, lists):
    rows[...] = jnp.zeros_like(rows)
    for k, ref in enumerate(lists):
        rows[k : k + 1, 0 : ref.shape[1]] = ref[...].astype(F32)
    turned = jnp.transpose(rows[...])[: lists[0].shape[1]]
    return [turned[:, k : k + 1] for k in range(len(lists))]


def on_even():
    return lax.rem(lax.axis_index("tile"), 2) == 0


def split(x):
    hi = x.astype(BF16)
    return hi, (x - hi.astype(F32)).astype(BF16)


def lanes(rows):
    return lax.broadcasted_iota(jnp.int32, (rows, 128), 1).astype(F32)


def hits(cells, row):
    return cells == lanes(cells.shape[0]) + jnp.asarray(row * 128, F32)


def kept(cells, weights, row):
    return 1.0 - jnp.sum(jnp.where(hits(cells, row), weights, 0.0), axis=0, keepdims=True)


def padded_levels(x):
    return jnp.concatenate([x, jnp.zeros((PAD - LEV, 128), F32)], axis=0)


def picked(fields, marks):
    hi, lo = split(fields)
    return lax.dot_general(
        jnp.concatenate([marks, marks], axis=1),
        jnp.concatenate([hi, lo], axis=1),
        (((1,), (1,)), ((), ())),
        preferred_element_type=F32,
    )


def feed_row(sums, weights, targets):
    wide = jnp.concatenate([sums * weights, jnp.zeros((sums.shape[0], 128 - MARK), F32)], axis=1)
    return jnp.where(lanes(sums.shape[0]) == float(MARK), targets, wide)


def stacked_matrix(slab):
    turned = jnp.transpose(slab)[:FULL, :]
    wide = jnp.concatenate([turned, jnp.zeros((FULL, 128 - FULL), F32)], axis=1)
    hi = wide.astype(BF16).astype(F32)
    lo = wide - hi
    return jnp.concatenate(
        [hi + pltpu.roll(hi, FULL, 1), lo + pltpu.roll(lo, FULL, 1)], axis=1
    ).astype(BF16)


def matrices_kernel(rows, inv_ref, out_ref, slab):
    slab[...] = jnp.zeros_like(slab)
    for r in range(rows):
        slab[0:LEV, 0:LEV] = inv_ref[pl.ds(r, LEV, stride=rows), :]
        out_ref[r] = stacked_matrix(slab[...])


def matrices(inv, rows):
    return pl.pallas_call(
        functools.partial(matrices_kernel, rows),
        out_shape=jax.ShapeDtypeStruct((rows, FULL, 256), BF16),
        scratch_shapes=[pltpu.VMEM((FULL, 128), F32)],
        compiler_params=pltpu.CompilerParams(vmem_limit_bytes=VMEM_LIMIT),
        name="matrices",
    )(inv)


def pack_row(ref, j, field, inv_ref, kappa_ref, row, rows, slab):
    slab[0:LEV, 0:LEV] = inv_ref[pl.ds(row, LEV, stride=rows), :]
    slab[FULL : FULL + 32] = slab[0:32] + pltpu.roll(slab[LEV // 2 : LEV // 2 + 32], 64, 1)
    for t in range(6):
        top = (6 * j + t) * PAD
        pad = top + LEV
        ref[top:pad] = field(t)
        if t < 5:
            ref[pad : pad + 5] = slab[FULL + 5 * t : FULL + 5 * t + 5]
            ref[pad + 5 : pad + 6] = jnp.zeros((1, 128), F32)
        else:
            ref[pad : pad + 1] = kappa_ref[pl.ds(row, 1), :]
            ref[pad + 1 : pad + 6] = jnp.zeros((5, 128), F32)


def unpacked_matrix(slabs, slab):
    half = LEV // 2
    slab[...] = jnp.zeros_like(slab)
    for t in range(5):
        slab[FULL + 5 * t : FULL + 5 * t + 5] = slabs(t)[LEV : LEV + 5]
    both = slab[FULL : FULL + 32]
    low = lax.broadcasted_iota(jnp.int32, both.shape, 1) < LEV
    slab[0:half] = jnp.where(low, both, 0.0)[:half]
    slab[half:LEV] = jnp.where(low, pltpu.roll(both, 64, 1), 0.0)[:half]
    return slab[0:FULL]


def prepare_kernel(halo, *refs):
    sources, refs = refs[:9], refs[9:]
    feed_ref, sib_ref, cross_ref, *refs = refs
    local, (names, slab, arrived) = refs[:9], refs[9:]
    copies = [
        pltpu.make_async_copy(source, target, arrived.at[k])
        for k, (source, target) in enumerate(zip(sources, local))
    ]
    for copy in copies:
        copy.start()
    lists, (lam_ref, inv_ref, kappa_ref) = local[:3], local[3:6]
    rows = kappa_ref.shape[0]
    for copy in copies[:4]:
        copy.wait()
    cells, targets, weights = columns(names, lists)

    def level_rows(t, r):
        return lam_ref[pl.ds(t * LEV * rows + r, LEV, stride=rows), :]

    marks = [jnp.where(hits(cells, r), 1.0, 0.0).astype(BF16) for r in range(rows)]
    for g in range(3):
        total = jnp.zeros((cells.shape[0], MARK), F32)
        for r in range(rows):
            both = [padded_levels(level_rows(2 * g + t, r)) for t in range(2)]
            total = total + picked(jnp.concatenate(both, axis=0), marks[r])
        row = feed_row(total, weights, targets)
        feed_ref[0, g] = row
        slots = row.shape[0]
        at = (halo + 1) * 6 * PAD + g * slots
        cross_ref[at : at + slots] = row
    slab[...] = jnp.zeros_like(slab)
    even = on_even()
    for copy in copies[4:]:
        copy.wait()
    for ref, head in ((sib_ref, ~even), (cross_ref, even)):
        r = jnp.where(head, 0, rows - 1)
        left = kept(cells, weights, r)
        field = lambda t: level_rows(t, r) * left
        pack_row(ref, halo, field, inv_ref, kappa_ref, r, rows, slab)
        child_ref, child_inv, child_kappa = local[6:9]
        crows = child_kappa.shape[0]
        for j in range(halo):
            r = jnp.where(head, j, crows - halo + j)
            field = lambda t: child_ref[pl.ds(t * LEV * crows + r, LEV, stride=crows), :]
            pack_row(ref, j, field, child_inv, child_kappa, r, crows, slab)


def prepare(lists, lam, inv, kappa, child, child_inv, child_kappa, halo):
    slots = lists[0].shape[1]
    edge = (halo + 1) * 6 * PAD
    operands = (*lists, lam, inv, kappa, child, child_inv, child_kappa)
    return pl.pallas_call(
        functools.partial(prepare_kernel, halo),
        in_specs=[pl.BlockSpec(memory_space=pltpu.HBM)] * len(operands),
        out_shape=(
            jax.ShapeDtypeStruct((1, 3, slots, 128), F32),
            jax.ShapeDtypeStruct((edge, 128), F32),
            jax.ShapeDtypeStruct((edge + 6 * slots, 128), F32),
        ),
        scratch_shapes=[pltpu.VMEM(x.shape, x.dtype) for x in operands]
        + [
            pltpu.VMEM((8, 128), F32),
            pltpu.VMEM((2 * FULL, 128), F32),
            pltpu.SemaphoreType.DMA((len(operands),)),
        ],
        compiler_params=pltpu.CompilerParams(vmem_limit_bytes=62 * 1024 * 1024),
        name="prepare",
    )(*operands)


def steps_kernel(rows, halo, steps, gather, places, *refs):
    lists, refs = refs[:3], refs[3:]
    feed_refs, refs = refs[: len(places)], refs[len(places) :]
    (lam_ref, sib_ref, cross_ref, mat_ref, kappa_ref), refs = refs[:5], refs[5:]
    if gather:
        out_ref, given_ref, *refs = refs
    else:
        (out_ref, *refs), given_ref = refs, None
    onehot, chosen, count, mats, coef, zbuf, names, slab, *ybufs = refs
    grown = rows + 2 * halo
    group = pl.program_id(0)
    even = on_even()
    cells, targets, weights = columns(names, lists)
    slots = targets.shape[0]
    units = sum(count for _, count in places)
    feeds = jnp.concatenate(
        [
            ref[pl.ds(pl.multiple_of(start + (3 * u + group) * slots, 8), slots), :]
            for ref, (start, count) in zip(feed_refs, places)
            for u in range(count)
        ],
        axis=0,
    )
    first_edge = 0 if gather else sib_ref.shape[0] // (6 * PAD) - 1

    def edge_row(ref, j, t):
        at = ((first_edge + j) * 6 + t) * PAD
        return ref[pl.ds(at if isinstance(at, int) else pl.multiple_of(at, 8), PAD), :]

    def low_row(j, t):
        return jnp.where(even, edge_row(cross_ref, j, t), edge_row(sib_ref, j, t))

    def high_row(j, t):
        return jnp.where(even, edge_row(sib_ref, j, t), edge_row(cross_ref, j, t))

    run = functools.partial(
        run_rows,
        rows,
        halo,
        steps,
        gather,
        group,
        lam_ref,
        low_row,
        high_row,
        (cells, targets, weights),
        (out_ref, given_ref),
        (mats, coef, zbuf, ybufs),
    )

    @pl.when(group == 0)
    def prepare():
        mats[halo : halo + rows] = mat_ref[...]
        kap = [None] * grown
        for j in range(halo):
            for q, row in ((j, low_row), (halo + rows + j, high_row)):
                slabs = functools.partial(row, j)
                mats[q] = stacked_matrix(unpacked_matrix(slabs, slab))
                kap[q] = slabs(5)[LEV : LEV + 1, :]
        for r in range(rows):
            kap[halo + r] = kappa_ref[r : r + 1, :]
        lane = lax.broadcasted_iota(jnp.int32, (1, 128), 1)
        for q in range(grown):
            k = kap[q]
            coef[0, q : q + 1, :] = k
            coef[1, q : q + 1, :] = jnp.where(lane == 0, 0.0, pltpu.roll(k, 1, 1))
            coef[2, q : q + 1, :] = jnp.where(lane == 127, 0.0, pltpu.roll(k, 127, 1))
            coef[3, q : q + 1, :] = 1.0 - 4.0 * k
        for r in range(rows):
            coef[4, r : r + 1, :] = kept(cells, weights, r)
        base = ((lax.axis_index("tile") * rows - halo) * 128).astype(F32)
        total = units * slots
        where = jnp.transpose(feeds)[MARK : MARK + 1, :] - base
        inside = jnp.where((where >= 0.0) & (where < float(grown * 128)), 1.0, 0.0)
        earlier = lax.broadcasted_iota(jnp.int32, (total, total), 0) < lax.broadcasted_iota(
            jnp.int32, (total, total), 1
        )
        place = jnp.dot(
            jnp.broadcast_to(inside, (16, total)).astype(BF16),
            jnp.where(earlier, 1.0, 0.0).astype(BF16),
            preferred_element_type=F32,
        )[0:1]
        place = jnp.where(inside > 0.0, place, -1.0)
        rank = lax.broadcasted_iota(jnp.int32, (FEW, total), 0).astype(F32)
        chosen[...] = jnp.where(rank == place, 1.0, 0.0).astype(BF16)
        count[0] = jnp.sum(inside).astype(jnp.int32)

        def mark(reached):
            for q in range(grown):
                onehot[q // 2, 0 : reached.shape[0], (q % 2) * 128 : (q % 2) * 128 + 128] = jnp.where(
                    hits(reached, q), 1.0, 0.0
                ).astype(BF16)

        @pl.when(count[0] <= FEW)
        def mark_few():
            cell = jnp.where(lanes(total) == float(MARK), feeds - base, 0.0)
            cell_hi, cell_lo = split(cell)
            reached = jnp.dot(chosen[...], cell_hi, preferred_element_type=F32)
            reached = reached + jnp.dot(chosen[...], cell_lo, preferred_element_type=F32)
            mark(reached[:, MARK : MARK + 1])

        @pl.when(count[0] > FEW)
        def mark_all():
            mark(feeds[:, MARK : MARK + 1] - base)

    feed_hi, feed_lo = split(feeds)

    @pl.when(count[0] <= FEW)
    def few():
        near = jnp.dot(
            chosen[...], jnp.concatenate([feed_hi, feed_lo], axis=1), preferred_element_type=F32
        )
        near = [jnp.transpose(near[:, k : k + 128])[:MARK, :].astype(BF16) for k in (0, 128)]
        left = jnp.concatenate(near, axis=1)

        def arrive(pair):
            marks = onehot[pair, 0:FEW, :]
            return jnp.dot(left, jnp.concatenate([marks, marks], axis=0), preferred_element_type=F32)

        run(arrive)

    @pl.when(count[0] > FEW)
    def many():
        turned = [jnp.transpose(x.astype(F32))[:MARK, :] for x in (feed_hi, feed_lo)]
        left = jnp.concatenate(turned, axis=0).astype(BF16)

        def arrive(pair):
            both = jnp.dot(left, onehot[pair], preferred_element_type=F32)
            return both[:MARK] + both[MARK:]

        run(arrive)


def run_rows(rows, halo, steps, gather, group, lam_ref, low_row, high_row, lists, outs, scratch, arrive):
    cells, targets, weights = lists
    mats, coef, zbuf, ybufs = scratch
    out_ref, given_ref = outs
    grown = rows + 2 * halo
    tail_rows = jnp.zeros((FULL - PAD, 256), F32)

    def store(q, z):
        hi, lo = split(jnp.concatenate([z, tail_rows], axis=0))
        zbuf[q, 0:FULL] = hi
        zbuf[q, FULL : 2 * FULL] = lo

    arrived = {}

    def start(q):
        if q % 2 == 0:
            arrived[q // 2] = arrive(q // 2)
        here = arrived[q // 2][:, (q % 2) * 128 : (q % 2) * 128 + 128]
        parts = []
        r = q - halo
        for t in range(2):
            if 0 <= r < rows:
                x = padded_levels(lam_ref[pl.ds(t * LEV * rows + r, LEV, stride=rows), :])
                if not gather:
                    x = x * coef[4, r : r + 1, :]
            else:
                at = 2 * group + t
                x = low_row(q, at) if q < halo else high_row(q - halo - rows, at)
            parts.append(x + here[t * PAD : (t + 1) * PAD])
        store(q, jnp.concatenate(parts, axis=1))

    def lift(k, q):
        z = zbuf[q]
        y = jnp.dot(mats[q][:, : 3 * FULL], jnp.concatenate([z, z[:FULL]], axis=0), preferred_element_type=F32)
        ybufs[k][q] = y[:PAD]

    def spread(k, q):
        parts = []
        for t in range(2):
            s = slice(t * 128, t * 128 + 128)
            y = ybufs[k][q, :, s]
            z = y * coef[3, q : q + 1, :]
            z = z + pltpu.roll(y, 1, 1) * coef[1, q : q + 1, :]
            z = z + pltpu.roll(y, 127, 1) * coef[2, q : q + 1, :]
            z = z + ybufs[k][q - 1, :, s] * coef[0, q - 1 : q, :]
            z = z + ybufs[k][q + 1, :, s] * coef[0, q + 1 : q + 2, :]
            parts.append(z)
        if k < steps - 1:
            store(q, jnp.concatenate(parts, axis=1))
            return
        r = q - halo
        for t in range(2):
            z = parts[t]
            if gather:
                z = z * coef[4, r : r + 1, :]
            out_ref[pl.ds(t * LEV * rows + r, LEV, stride=rows), :] = z[:LEV]
        if gather:
            marks = jnp.where(hits(cells, r), 1.0, 0.0).astype(BF16)
            totals.append(picked(jnp.concatenate(parts, axis=0), marks))
            if len(totals) == 2:
                totals[:] = [totals[0] + totals[1]]

    totals = []
    plan = []
    for q in range(grown):
        plan.append((q, 0, start, (q,)))
        for k in range(steps):
            if k <= q < grown - k:
                plan.append((q + 5 + 12 * k, 1 + 2 * k, lift, (k, q)))
            if k + 1 <= q < grown - k - 1:
                plan.append((q + 12 + 12 * k, 2 + 2 * k, spread, (k, q)))
    for _, _, act, args in sorted(plan, key=lambda p: p[:2]):
        act(*args)
    if gather:
        given_ref[0, 0] = feed_row(totals[0], weights, targets)


def run_steps(lists, feeds, lam, sib, cross, mats, kappa, halo, steps, gather):
    rows = kappa.shape[0]
    grown = rows + 2 * halo
    slots = lists[0].shape[1]
    places = tuple((start, count) for _, start, count in feeds)
    feeds = [x for x, _, _ in feeds]
    units = sum(count for _, count in places)
    whole = lambda x: pl.BlockSpec(x.shape, lambda g: (0,) * x.ndim)
    field = pl.BlockSpec((2 * LEV * rows, 128), lambda g: (g, 0))
    out_shape = [jax.ShapeDtypeStruct(lam.shape, F32)]
    out_specs = [field]
    if gather:
        out_shape.append(jax.ShapeDtypeStruct((1, 3, slots, 128), F32))
        out_specs.append(pl.BlockSpec((1, 1, slots, 128), lambda g: (0, g, 0, 0)))
    return pl.pallas_call(
        functools.partial(steps_kernel, rows, halo, steps, gather, places),
        grid=(3,),
        in_specs=[whole(x) for x in (*lists, *feeds)]
        + [field, whole(sib), whole(cross), whole(mats), whole(kappa)],
        out_specs=out_specs,
        out_shape=out_shape,
        scratch_shapes=[
            pltpu.VMEM((grown // 2, units * slots, 256), BF16),
            pltpu.VMEM((FEW, units * slots), BF16),
            pltpu.SMEM((1,), jnp.int32),
            pltpu.VMEM((grown, FULL, 256), BF16),
            pltpu.VMEM((5, (grown + 7) // 8 * 8, 128), F32),
            pltpu.VMEM((grown, 2 * FULL, 256), BF16),
            pltpu.VMEM((8, 128), F32),
            pltpu.VMEM((2 * FULL, 128), F32),
        ]
        + [pltpu.VMEM((grown, PAD, 256), F32) for _ in range(steps)],
        compiler_params=pltpu.CompilerParams(vmem_limit_bytes=VMEM_LIMIT),
        name="child" if gather else "parent",
    )(*lists, *feeds, lam, sib, cross, mats, kappa)


def exchange(x, pairs):
    return lax.ppermute(x, "tile", [p for a, b in pairs for p in ((a, b), (b, a))])


def sibling(x):
    return exchange(x, [(i, i + 1) for i in range(0, lax.axis_size("tile"), 2)])


def beyond(x, chips):
    count = lax.axis_size("tile")
    first, distance = (1, 1) if chips == 1 else (0, 2 * chips + 1)
    return exchange(x, [(i, i + distance) for i in range(first, count - distance, 2)])


def rows_of(x):
    return x.reshape(-1, 128)


def per_device(
    lam_parent,
    lam_child,
    kappa_parent,
    kappa_child,
    inv_parent,
    inv_child,
    bnd_child,
    bnd_parent,
    bnd_weight,
    upd_parent,
    upd_child,
    upd_weight,
):
    upd = [x.reshape(1, -1) for x in (upd_parent, upd_child, upd_weight)]
    bnd = [x.reshape(1, -1) for x in (bnd_child, bnd_parent, bnd_weight)]
    flat_parent = lam_parent.reshape(-1, 128)
    flat_child = lam_child.reshape(-1, 128)
    inv_parent, inv_child = (
        jnp.transpose(x, (1, 0, 2)).reshape(-1, x.shape[2]) for x in (inv_parent, inv_child)
    )
    feed, to_sib, to_cross = prepare(
        upd, flat_parent, inv_parent, kappa_parent, flat_child, inv_child, kappa_child, 3
    )
    slots = bnd_child.shape[0]
    unit = 3 * slots

    beside = sibling(feed)
    last = to_cross.shape[0] - unit
    to_cross = lax.dynamic_update_slice(to_cross, rows_of(beside), (last, 0))
    far = beyond(beside, 3)
    chip = jnp.concatenate([feed, beside], axis=0)
    two = beyond(chip, 2)
    cross = beyond(to_cross, 1)
    fetched = jnp.concatenate([cross[last - unit :], rows_of(two), rows_of(far)], axis=0)
    feeds = [(rows_of(chip), 0, 2), (fetched, 0, 4), (sibling(fetched), 0, 5)]
    sib = sibling(to_sib)
    adj_child, given = run_steps(
        bnd, feeds, flat_child, sib, cross, matrices(inv_child, kappa_child.shape[0]), kappa_child, 3, 3, True
    )
    beside = sibling(given)
    chip = jnp.concatenate([given, beside], axis=0)
    fetched = jnp.concatenate([beyond(chip, 1), beyond(chip, 2), beyond(beside, 3)], axis=0)
    feeds = [(rows_of(chip), 0, 2), (rows_of(fetched), 0, 4), (rows_of(sibling(fetched)), 0, 5)]
    (adj_parent,) = run_steps(
        upd, feeds, flat_parent, sib, cross, matrices(inv_parent, kappa_parent.shape[0]), kappa_parent, 1, 1, False
    )
    return adj_parent.reshape(lam_parent.shape), adj_child.reshape(lam_child.shape)


def solution(mesh):
    field, plane = P(None, None, "tile", None), P("tile", None)
    cube, line = P("tile", None, None), P("tile")
    in_specs = (field, field, plane, plane, cube, cube) + (line,) * 6
    return jax.shard_map(
        per_device, mesh=mesh, in_specs=in_specs, out_specs=(field, field), check_vma=False
    )
```

```python
import functools

import jax
import jax.numpy as jnp
from jax import lax
from jax.experimental import pallas as pl
from jax.experimental.pallas import tpu as pltpu
from jax.sharding import PartitionSpec as P

F32, BF16 = jnp.float32, jnp.bfloat16
LEV, PAD, FULL = 50, 56, 64
FEW = 128
MARK = 2 * PAD
VMEM_LIMIT = 32 * 1024 * 1024


def columns(rows, lists):
    rows[...] = jnp.zeros_like(rows)
    for k, ref in enumerate(lists):
        rows[k : k + 1, 0 : ref.shape[1]] = ref[...].astype(F32)
    turned = jnp.transpose(rows[...])[: lists[0].shape[1]]
    return [turned[:, k : k + 1] for k in range(len(lists))]


def on_even():
    return lax.rem(lax.axis_index("tile"), 2) == 0


def split(x):
    hi = x.astype(BF16)
    return hi, (x - hi.astype(F32)).astype(BF16)


def lanes(rows):
    return lax.broadcasted_iota(jnp.int32, (rows, 128), 1).astype(F32)


def hits(cells, row):
    return cells == lanes(cells.shape[0]) + jnp.asarray(row * 128, F32)


def kept(cells, weights, row):
    return 1.0 - jnp.sum(jnp.where(hits(cells, row), weights, 0.0), axis=0, keepdims=True)


def padded_levels(x):
    return jnp.concatenate([x, jnp.zeros((PAD - LEV, 128), F32)], axis=0)


def picked(fields, marks):
    hi, lo = split(fields)
    return lax.dot_general(
        jnp.concatenate([marks, marks], axis=1),
        jnp.concatenate([hi, lo], axis=1),
        (((1,), (1,)), ((), ())),
        preferred_element_type=F32,
    )


def feed_row(sums, weights, targets):
    wide = jnp.concatenate([sums * weights, jnp.zeros((sums.shape[0], 128 - MARK), F32)], axis=1)
    return jnp.where(lanes(sums.shape[0]) == float(MARK), targets, wide)


def stacked_matrix(slab):
    turned = jnp.transpose(slab)[:FULL, :]
    wide = jnp.concatenate([turned, jnp.zeros((FULL, 128 - FULL), F32)], axis=1)
    hi = wide.astype(BF16).astype(F32)
    lo = wide - hi
    return jnp.concatenate(
        [hi + pltpu.roll(hi, FULL, 1), lo + pltpu.roll(lo, FULL, 1)], axis=1
    ).astype(BF16)


def stage_kernel(rows, *refs):
    lists, refs = refs[:3], refs[3:]
    inv_ref, kappa_ref, lam_ref, mats_ref, field_ref, small_ref, names, slab, arrived = refs
    copy = pltpu.make_async_copy(lam_ref, field_ref, arrived)
    copy.start()
    slots = lists[0].shape[1]
    lane = lax.broadcasted_iota(jnp.int32, (slots, 128), 1)
    small = jnp.zeros((slots, 128), F32)
    for k, column in enumerate(columns(names, lists)):
        small = jnp.where(lane == k, column, small)
    small_ref[0:slots] = small
    small_ref[slots : slots + rows] = kappa_ref[...]
    slab[...] = jnp.zeros_like(slab)
    for r in range(rows):
        slab[0:LEV, 0:LEV] = inv_ref[pl.ds(r, LEV, stride=rows), :]
        mats_ref[r] = stacked_matrix(slab[...])
    copy.wait()


def stage(lists, inv, kappa, lam):
    rows = kappa.shape[0]
    return pl.pallas_call(
        functools.partial(stage_kernel, rows),
        in_specs=[pl.BlockSpec(memory_space=pltpu.VMEM)] * 5 + [pl.BlockSpec(memory_space=pl.ANY)],
        out_shape=(
            jax.ShapeDtypeStruct((rows, FULL, 256), BF16),
            jax.ShapeDtypeStruct(lam.shape, F32),
            jax.ShapeDtypeStruct((lists[0].shape[1] + rows, 128), F32),
        ),
        scratch_shapes=[
            pltpu.VMEM((8, 128), F32),
            pltpu.VMEM((FULL, 128), F32),
            pltpu.SemaphoreType.DMA(()),
        ],
        compiler_params=pltpu.CompilerParams(vmem_limit_bytes=VMEM_LIMIT),
        name="stage",
    )(*lists, inv, kappa, lam)


def gathered_kernel(one_ref, two_ref, three_ref, ready_ref, out_ref):
    out_ref[0:2] = one_ref[...]
    out_ref[2:4] = two_ref[...]
    out_ref[4:5] = three_ref[...]


def gathered(one, two, three, ready):
    return pl.pallas_call(
        gathered_kernel,
        in_specs=[pl.BlockSpec(memory_space=pltpu.VMEM)] * 3 + [pl.BlockSpec(memory_space=pl.ANY)],
        out_shape=jax.ShapeDtypeStruct((5, *one.shape[1:]), F32),
        compiler_params=pltpu.CompilerParams(vmem_limit_bytes=VMEM_LIMIT),
        name="gathered",
    )(one, two, three, ready)


def pack_row(ref, j, field, inv_ref, kappa_ref, row, rows, slab):
    slab[0:LEV, 0:LEV] = inv_ref[pl.ds(row, LEV, stride=rows), :]
    slab[FULL : FULL + 32] = slab[0:32] + pltpu.roll(slab[LEV // 2 : LEV // 2 + 32], 64, 1)
    for t in range(6):
        top = (6 * j + t) * PAD
        pad = top + LEV
        ref[top:pad] = field(t)
        if t < 5:
            ref[pad : pad + 5] = slab[FULL + 5 * t : FULL + 5 * t + 5]
            ref[pad + 5 : pad + 6] = jnp.zeros((1, 128), F32)
        else:
            ref[pad : pad + 1] = kappa_ref[pl.ds(row, 1), :]
            ref[pad + 1 : pad + 6] = jnp.zeros((5, 128), F32)


def unpacked_matrix(slabs, slab):
    half = LEV // 2
    slab[...] = jnp.zeros_like(slab)
    for t in range(5):
        slab[FULL + 5 * t : FULL + 5 * t + 5] = slabs(t)[LEV : LEV + 5]
    both = slab[FULL : FULL + 32]
    low = lax.broadcasted_iota(jnp.int32, both.shape, 1) < LEV
    slab[0:half] = jnp.where(low, both, 0.0)[:half]
    slab[half:LEV] = jnp.where(low, pltpu.roll(both, 64, 1), 0.0)[:half]
    return slab[0:FULL]


def prepare_kernel(halo, *refs):
    sources, refs = refs[:9], refs[9:]
    feed_ref, sib_ref, cross_ref, *refs = refs
    local, (names, slab, arrived) = refs[:9], refs[9:]
    copies = [
        pltpu.make_async_copy(source, target, arrived.at[k])
        for k, (source, target) in enumerate(zip(sources, local))
    ]
    for copy in copies:
        copy.start()
    lists, (lam_ref, inv_ref, kappa_ref) = local[:3], local[3:6]
    rows = kappa_ref.shape[0]
    for copy in copies[:4]:
        copy.wait()
    cells, targets, weights = columns(names, lists)

    def level_rows(t, r):
        return lam_ref[pl.ds(t * LEV * rows + r, LEV, stride=rows), :]

    marks = [jnp.where(hits(cells, r), 1.0, 0.0).astype(BF16) for r in range(rows)]
    for g in range(3):
        total = jnp.zeros((cells.shape[0], MARK), F32)
        for r in range(rows):
            both = [padded_levels(level_rows(2 * g + t, r)) for t in range(2)]
            total = total + picked(jnp.concatenate(both, axis=0), marks[r])
        feed_ref[0, g] = feed_row(total, weights, targets)
    slab[...] = jnp.zeros_like(slab)
    even = on_even()
    for copy in copies[4:]:
        copy.wait()
    for ref, head in ((sib_ref, ~even), (cross_ref, even)):
        r = jnp.where(head, 0, rows - 1)
        left = kept(cells, weights, r)
        field = lambda t: level_rows(t, r) * left
        pack_row(ref, halo, field, inv_ref, kappa_ref, r, rows, slab)
        child_ref, child_inv, child_kappa = local[6:9]
        crows = child_kappa.shape[0]
        for j in range(halo):
            r = jnp.where(head, j, crows - halo + j)
            field = lambda t: child_ref[pl.ds(t * LEV * crows + r, LEV, stride=crows), :]
            pack_row(ref, j, field, child_inv, child_kappa, r, crows, slab)


def prepare(lists, lam, inv, kappa, child, child_inv, child_kappa, halo):
    slots = lists[0].shape[1]
    edge = (halo + 1) * 6 * PAD
    operands = (*lists, lam, inv, kappa, child, child_inv, child_kappa)
    return pl.pallas_call(
        functools.partial(prepare_kernel, halo),
        in_specs=[pl.BlockSpec(memory_space=pltpu.HBM)] * len(operands),
        out_shape=(
            jax.ShapeDtypeStruct((1, 3, slots, 128), F32),
            jax.ShapeDtypeStruct((edge, 128), F32),
            jax.ShapeDtypeStruct((edge, 128), F32),
        ),
        scratch_shapes=[pltpu.VMEM(x.shape, x.dtype) for x in operands]
        + [
            pltpu.VMEM((8, 128), F32),
            pltpu.VMEM((2 * FULL, 128), F32),
            pltpu.SemaphoreType.DMA((len(operands),)),
        ],
        compiler_params=pltpu.CompilerParams(vmem_limit_bytes=62 * 1024 * 1024),
        name="prepare",
    )(*operands)


def steps_kernel(rows, halo, steps, gather, places, *refs):
    feed_refs, refs = refs[: len(places)], refs[len(places) :]
    (small_ref, lam_ref, sib_ref, cross_ref, mat_ref), refs = refs[:5], refs[5:]
    if gather:
        out_ref, given_ref, *refs = refs
    else:
        (out_ref, *refs), given_ref = refs, None
    onehot, chosen, count, edge_mats, coef, held, sent, slab, zbuf, *ybufs = refs
    grown = rows + 2 * halo
    even = on_even()
    slots = small_ref.shape[0] - rows
    cells, targets, weights = (small_ref[0:slots, k : k + 1] for k in range(3))
    units = sum(n for _, n in places)
    total = units * slots
    first_edge = 0 if gather else sib_ref.shape[0] // (6 * PAD) - 1

    def aligned(start, size):
        return pl.ds(start if isinstance(start, int) else pl.multiple_of(start, 8), size)

    def feeds_of(group):
        return jnp.concatenate(
            [
                ref[aligned(start + (3 * u + group) * slots, slots), :]
                for ref, (start, n) in zip(feed_refs, places)
                for u in range(n)
            ],
            axis=0,
        )

    def edge_row(ref, j, t):
        return ref[aligned(((first_edge + j) * 6 + t) * PAD, PAD), :]

    def low_row(j, t):
        return jnp.where(even, edge_row(cross_ref, j, t), edge_row(sib_ref, j, t))

    def high_row(j, t):
        return jnp.where(even, edge_row(sib_ref, j, t), edge_row(cross_ref, j, t))

    def matrix(q):
        if halo <= q < halo + rows:
            return mat_ref[q - halo]
        return edge_mats[q if q < halo else q - rows]

    kap = [None] * grown
    for j in range(halo):
        for q, row in ((j, low_row), (halo + rows + j, high_row)):
            slabs = functools.partial(row, j)
            edge_mats[q if q < halo else q - rows] = stacked_matrix(unpacked_matrix(slabs, slab))
            kap[q] = slabs(5)[LEV : LEV + 1, :]
    for r in range(rows):
        kap[halo + r] = small_ref[slots + r : slots + r + 1, :]
    lane = lax.broadcasted_iota(jnp.int32, (1, 128), 1)
    for q in range(grown):
        k = kap[q]
        coef[0, q : q + 1, :] = k
        coef[1, q : q + 1, :] = jnp.where(lane == 0, 0.0, pltpu.roll(k, 1, 1))
        coef[2, q : q + 1, :] = jnp.where(lane == 127, 0.0, pltpu.roll(k, 127, 1))
        coef[3, q : q + 1, :] = 1.0 - 4.0 * k
    for r in range(rows):
        coef[4, r : r + 1, :] = kept(cells, weights, r)

    base = ((lax.axis_index("tile") * rows - halo) * 128).astype(F32)
    any_feeds = feeds_of(0)
    where = jnp.transpose(any_feeds)[MARK : MARK + 1, :] - base
    inside = jnp.where((where >= 0.0) & (where < float(grown * 128)), 1.0, 0.0)
    earlier = lax.broadcasted_iota(jnp.int32, (total, total), 0) < lax.broadcasted_iota(
        jnp.int32, (total, total), 1
    )
    place = jnp.dot(
        jnp.broadcast_to(inside, (16, total)).astype(BF16),
        jnp.where(earlier, 1.0, 0.0).astype(BF16),
        preferred_element_type=F32,
    )[0:1]
    place = jnp.where(inside > 0.0, place, -1.0)
    rank = lax.broadcasted_iota(jnp.int32, (FEW, total), 0).astype(F32)
    chosen[...] = jnp.where(rank == place, 1.0, 0.0).astype(BF16)
    count[0] = jnp.sum(inside).astype(jnp.int32)

    def mark(reached):
        for q in range(grown):
            onehot[q // 2, 0 : reached.shape[0], (q % 2) * 128 : (q % 2) * 128 + 128] = jnp.where(
                hits(reached, q), 1.0, 0.0
            ).astype(BF16)

    def start_few(group):
        feed_hi, feed_lo = split(feeds_of(group))
        near = jnp.dot(
            chosen[...], jnp.concatenate([feed_hi, feed_lo], axis=1), preferred_element_type=F32
        )
        near = [jnp.transpose(near[:, k : k + 128])[:MARK, :].astype(BF16) for k in (0, 128)]
        left = jnp.concatenate(near, axis=1)

        def arrive(pair):
            marks = onehot[pair, 0:FEW, :]
            return jnp.dot(left, jnp.concatenate([marks, marks], axis=0), preferred_element_type=F32)

        return arrive

    def start_many(group):
        turned = [jnp.transpose(x.astype(F32))[:MARK, :] for x in split(feeds_of(group))]
        left = jnp.concatenate(turned, axis=0).astype(BF16)

        def arrive(pair):
            both = jnp.dot(left, onehot[pair], preferred_element_type=F32)
            return both[:MARK] + both[MARK:]

        return arrive

    def copy_out(group):
        size = 2 * LEV * rows
        return pltpu.make_async_copy(
            held.at[group], out_ref.at[aligned(group * size, size), :], sent.at[group]
        )

    def finish(group, totals):
        if gather:
            given_ref[0, group] = feed_row(totals[0], weights, targets)
        copy_out(group).start()

    def plan_of(at, group, arrive):
        arrived, totals = {}, []
        tail_rows = jnp.zeros((FULL - PAD, 256), F32)

        def store(q, z):
            hi, lo = split(jnp.concatenate([z, tail_rows], axis=0))
            zbuf[at, q, 0:FULL] = hi
            zbuf[at, q, FULL : 2 * FULL] = lo

        def begin(q):
            if q % 2 == 0:
                arrived[q // 2] = arrive(q // 2)
            here = arrived[q // 2][:, (q % 2) * 128 : (q % 2) * 128 + 128]
            parts = []
            r = q - halo
            for t in range(2):
                tracer = 2 * group + t
                if 0 <= r < rows:
                    x = lam_ref[pl.ds(tracer * LEV * rows + r, LEV, stride=rows), :]
                    x = padded_levels(x)
                    if not gather:
                        x = x * coef[4, r : r + 1, :]
                else:
                    x = low_row(q, tracer) if q < halo else high_row(q - halo - rows, tracer)
                parts.append(x + here[t * PAD : (t + 1) * PAD])
            store(q, jnp.concatenate(parts, axis=1))

        def lift(k, q):
            z = zbuf[at, q]
            y = jnp.dot(
                matrix(q)[:, : 3 * FULL],
                jnp.concatenate([z, z[:FULL]], axis=0),
                preferred_element_type=F32,
            )
            ybufs[k][at, q] = y[:PAD]

        def spread(k, q):
            parts = []
            for t in range(2):
                s = slice(t * 128, t * 128 + 128)
                y = ybufs[k][at, q, :, s]
                z = y * coef[3, q : q + 1, :]
                z = z + pltpu.roll(y, 1, 1) * coef[1, q : q + 1, :]
                z = z + pltpu.roll(y, 127, 1) * coef[2, q : q + 1, :]
                z = z + ybufs[k][at, q - 1, :, s] * coef[0, q - 1 : q, :]
                z = z + ybufs[k][at, q + 1, :, s] * coef[0, q + 1 : q + 2, :]
                parts.append(z)
            if k < steps - 1:
                store(q, jnp.concatenate(parts, axis=1))
                return
            r = q - halo
            for t in range(2):
                z = parts[t]
                if gather:
                    z = z * coef[4, r : r + 1, :]
                held[group, pl.ds(t * LEV * rows + r, LEV, stride=rows), :] = z[:LEV]
            if gather:
                marks = jnp.where(hits(cells, r), 1.0, 0.0).astype(BF16)
                totals.append(picked(jnp.concatenate(parts, axis=0), marks))
                if len(totals) == 2:
                    totals[:] = [totals[0] + totals[1]]

        plan = []
        for q in range(grown):
            plan.append((q, 0, functools.partial(begin, q)))
            for k in range(steps):
                if k <= q < grown - k:
                    plan.append((q + 5 + 12 * k, 1 + 2 * k, functools.partial(lift, k, q)))
                if k + 1 <= q < grown - k - 1:
                    plan.append((q + 12 + 12 * k, 2 + 2 * k, functools.partial(spread, k, q)))
        plan.append((grown + 12 * steps + 1, 0, functools.partial(finish, group, totals)))
        return plan

    def run(start):
        if gather:

            def pair(group, _):
                for _, _, act in sorted(plan_of(0, group, start(group)), key=lambda p: p[:2]):
                    act()
                return 0

            lax.fori_loop(0, 3, pair, 0)
        else:
            plan = [p for g in range(3) for p in plan_of(g, g, start(g))]
            for _, _, act in sorted(plan, key=lambda p: p[:2]):
                act()

    @pl.when(count[0] <= FEW)
    def few():
        cell = jnp.where(lanes(total) == float(MARK), any_feeds - base, 0.0)
        cell_hi, cell_lo = split(cell)
        reached = jnp.dot(chosen[...], cell_hi, preferred_element_type=F32)
        reached = reached + jnp.dot(chosen[...], cell_lo, preferred_element_type=F32)
        mark(reached[:, MARK : MARK + 1])
        run(start_few)

    @pl.when(count[0] > FEW)
    def many():
        mark(any_feeds[:, MARK : MARK + 1] - base)
        run(start_many)

    for group in range(3):
        copy_out(group).wait()


def run_steps(small, feeds, lam, sib, cross, mats, halo, steps, gather):
    rows = mats.shape[0]
    grown = rows + 2 * halo
    slots = small.shape[0] - rows
    places = tuple((start, n) for _, start, n in feeds)
    units = sum(n for _, n in places)
    near = pl.BlockSpec(memory_space=pltpu.VMEM)
    out_shape = [jax.ShapeDtypeStruct(lam.shape, F32)]
    out_specs = [pl.BlockSpec(memory_space=pl.ANY)]
    if gather:
        out_shape.append(jax.ShapeDtypeStruct((1, 3, slots, 128), F32))
        out_specs.append(near)
    lots = 1 if gather else 3
    return pl.pallas_call(
        functools.partial(steps_kernel, rows, halo, steps, gather, places),
        in_specs=[near] * (len(feeds) + 5),
        out_specs=out_specs,
        out_shape=out_shape,
        scratch_shapes=[
            pltpu.VMEM((grown // 2, units * slots, 256), BF16),
            pltpu.VMEM((FEW, units * slots), BF16),
            pltpu.SMEM((1,), jnp.int32),
            pltpu.VMEM((2 * halo, FULL, 256), BF16),
            pltpu.VMEM((5, (grown + 7) // 8 * 8, 128), F32),
            pltpu.VMEM((3, 2 * LEV * rows, 128), F32),
            pltpu.SemaphoreType.DMA((3,)),
            pltpu.VMEM((2 * FULL, 128), F32),
            pltpu.VMEM((lots, grown, 2 * FULL, 256), BF16),
        ]
        + [pltpu.VMEM((lots, grown, PAD, 256), F32) for _ in range(steps)],
        compiler_params=pltpu.CompilerParams(vmem_limit_bytes=VMEM_LIMIT),
        name="child" if gather else "parent",
    )(*[x for x, _, _ in feeds], small, lam, sib, cross, mats)


def exchange(x, pairs):
    return lax.ppermute(x, "tile", [p for a, b in pairs for p in ((a, b), (b, a))])


def sibling(x):
    return exchange(x, [(i, i + 1) for i in range(0, lax.axis_size("tile"), 2)])


def beyond(x, chips):
    count = lax.axis_size("tile")
    first, distance = (1, 1) if chips == 1 else (0, 2 * chips + 1)
    return exchange(x, [(i, i + distance) for i in range(first, count - distance, 2)])


def rows_of(x):
    return x.reshape(-1, 128)


def per_device(
    lam_parent,
    lam_child,
    kappa_parent,
    kappa_child,
    inv_parent,
    inv_child,
    bnd_child,
    bnd_parent,
    bnd_weight,
    upd_parent,
    upd_child,
    upd_weight,
):
    upd = [x.reshape(1, -1) for x in (upd_parent, upd_child, upd_weight)]
    bnd = [x.reshape(1, -1) for x in (bnd_child, bnd_parent, bnd_weight)]
    flat_parent = lam_parent.reshape(-1, 128)
    flat_child = lam_child.reshape(-1, 128)
    inv_parent, inv_child = (
        jnp.transpose(x, (1, 0, 2)).reshape(-1, x.shape[2]) for x in (inv_parent, inv_child)
    )
    feed, to_sib, to_cross = prepare(
        upd, flat_parent, inv_parent, kappa_parent, flat_child, inv_child, kappa_child, 3
    )
    cross, sib = beyond(to_cross, 1), sibling(to_sib)

    def all_near(own, ready):
        beside = sibling(own)
        chip = jnp.concatenate([own, beside], axis=0)
        fetched = gathered(beyond(chip, 1), beyond(chip, 2), beyond(beside, 3), ready)
        return [(rows_of(chip), 0, 2), (rows_of(fetched), 0, 4), (rows_of(sibling(fetched)), 0, 5)]

    mats, field, small = stage(bnd, inv_child, kappa_child, flat_child)
    adj_child, given = run_steps(small, all_near(feed, mats), field, sib, cross, mats, 3, 3, True)
    mats, field, small = stage(upd, inv_parent, kappa_parent, flat_parent)
    (adj_parent,) = run_steps(small, all_near(given, mats), field, sib, cross, mats, 1, 1, False)
    return adj_parent.reshape(lam_parent.shape), adj_child.reshape(lam_child.shape)


def solution(mesh):
    field, plane = P(None, None, "tile", None), P("tile", None)
    cube, line = P("tile", None, None), P("tile")
    in_specs = (field, field, plane, plane, cube, cube) + (line,) * 6
    return jax.shard_map(
        per_device, mesh=mesh, in_specs=in_specs, out_specs=(field, field), check_vma=False
    )
```

```python
import functools

import jax
import jax.numpy as jnp
from jax import lax
from jax.experimental import pallas as pl
from jax.experimental.pallas import tpu as pltpu
from jax.sharding import PartitionSpec as P

F32, BF16 = jnp.float32, jnp.bfloat16
LEV, PAD, FULL = 50, 56, 64
FEW = 128
MARK = 2 * PAD
VMEM_LIMIT = 32 * 1024 * 1024


def columns(rows, lists):
    rows[...] = jnp.zeros_like(rows)
    for k, ref in enumerate(lists):
        rows[k : k + 1, 0 : ref.shape[1]] = ref[...].astype(F32)
    turned = jnp.transpose(rows[...])[: lists[0].shape[1]]
    return [turned[:, k : k + 1] for k in range(len(lists))]


def on_even():
    return lax.rem(lax.axis_index("tile"), 2) == 0


def split(x):
    hi = x.astype(BF16)
    return hi, (x - hi.astype(F32)).astype(BF16)


def lanes(rows):
    return lax.broadcasted_iota(jnp.int32, (rows, 128), 1).astype(F32)


def hits(cells, row):
    return cells == lanes(cells.shape[0]) + jnp.asarray(row * 128, F32)


def kept(cells, weights, row):
    return 1.0 - jnp.sum(jnp.where(hits(cells, row), weights, 0.0), axis=0, keepdims=True)


def padded_levels(x):
    return jnp.concatenate([x, jnp.zeros((PAD - LEV, 128), F32)], axis=0)


def picked(fields, marks):
    hi, lo = split(fields)
    return lax.dot_general(
        jnp.concatenate([marks, marks], axis=1),
        jnp.concatenate([hi, lo], axis=1),
        (((1,), (1,)), ((), ())),
        preferred_element_type=F32,
    )


def feed_row(sums, weights, *targets):
    row = jnp.concatenate([sums * weights, jnp.zeros((sums.shape[0], 128 - MARK), F32)], axis=1)
    for k, target in enumerate(targets):
        row = jnp.where(lanes(sums.shape[0]) == float(MARK + k), target, row)
    return row


def stacked_matrix(slab):
    turned = jnp.transpose(slab)[:FULL, :]
    wide = jnp.concatenate([turned, jnp.zeros((FULL, 128 - FULL), F32)], axis=1)
    hi = wide.astype(BF16).astype(F32)
    lo = wide - hi
    return jnp.concatenate(
        [hi + pltpu.roll(hi, FULL, 1), lo + pltpu.roll(lo, FULL, 1)], axis=1
    ).astype(BF16)


def stage_kernel(rows, halo, places, *refs):
    lists, refs = refs[:3], refs[3:]
    (inv_ref, kappa_ref, lam_ref), refs = refs[:3], refs[3:]
    feed_refs, refs = refs[: len(places)], refs[len(places) :]
    if places:
        cross_ref, sib_ref, *refs = refs
    mats_ref, field_ref, small_ref, *refs = refs
    ready, (names, slab, arrived) = refs[:-3], refs[-3:]
    copy = pltpu.make_async_copy(lam_ref, field_ref, arrived)
    copy.start()
    slots = lists[0].shape[1]
    lane = lax.broadcasted_iota(jnp.int32, (slots, 128), 1)
    small = jnp.zeros((slots, 128), F32)
    for k, column in enumerate(columns(names, lists)):
        small = jnp.where(lane == k, column, small)
    small_ref[0:slots] = small
    small_ref[slots : slots + rows] = kappa_ref[...]
    slab[...] = jnp.zeros_like(slab)
    for r in range(rows):
        slab[0:LEV, 0:LEV] = inv_ref[pl.ds(r, LEV, stride=rows), :]
        mats_ref[r] = stacked_matrix(slab[0:FULL])
    if places:
        *ready, count_ref = ready
        readers = edge_readers(sib_ref.shape[0] // (6 * PAD) - halo, cross_ref, sib_ref)
        feeds = feeds_of(0, feed_refs, places, slots)
        count = set_up(rows, halo, MARK + 1, feeds, small_ref, readers, *ready, slab)
        count_ref[...] = jnp.zeros_like(count_ref) + count.astype(F32)
    copy.wait()


def stage(lists, inv, kappa, lam, halo=0, feeds=(), edges=()):
    rows = kappa.shape[0]
    slots = lists[0].shape[1]
    places = tuple((start, n) for _, start, n in feeds)
    near, shape = pl.BlockSpec(memory_space=pltpu.VMEM), jax.ShapeDtypeStruct
    extra = []
    if feeds:
        total = sum(n for _, n in places) * slots
        extra = [shape(*x) for x in set_up_shapes(rows, halo, total)] + [shape((8, 128), F32)]
    operands = [x for x, _, _ in feeds] + list(edges)
    return pl.pallas_call(
        functools.partial(stage_kernel, rows, halo, places),
        in_specs=[near] * 5 + [pl.BlockSpec(memory_space=pl.ANY)] + [near] * len(operands),
        out_shape=[
            shape((rows, FULL, 256), BF16),
            shape(lam.shape, F32),
            shape((slots + rows, 128), F32),
            *extra,
        ],
        scratch_shapes=[
            pltpu.VMEM((8, 128), F32),
            pltpu.VMEM((2 * FULL, 128), F32),
            pltpu.SemaphoreType.DMA(()),
        ],
        compiler_params=pltpu.CompilerParams(vmem_limit_bytes=VMEM_LIMIT),
        name="stage",
    )(*lists, inv, kappa, lam, *operands)


def gathered_kernel(three_ref, two_ref, one_ref, ready_ref, out_ref):
    out_ref[0:2] = one_ref[...]
    out_ref[2:4] = two_ref[...]
    out_ref[4:5] = three_ref[...]


def gathered(three, two, one, ready):
    return pl.pallas_call(
        gathered_kernel,
        in_specs=[pl.BlockSpec(memory_space=pltpu.VMEM)] * 3 + [pl.BlockSpec(memory_space=pl.ANY)],
        out_shape=jax.ShapeDtypeStruct((5, *one.shape[1:]), F32),
        compiler_params=pltpu.CompilerParams(vmem_limit_bytes=VMEM_LIMIT),
        name="gathered",
    )(three, two, one, ready)


def pack_row(ref, j, field, inv_ref, kappa_ref, row, rows, slab):
    slab[0:LEV, 0:LEV] = inv_ref[pl.ds(row, LEV, stride=rows), :]
    slab[FULL : FULL + 32] = slab[0:32] + pltpu.roll(slab[LEV // 2 : LEV // 2 + 32], 64, 1)
    for t in range(6):
        top = (6 * j + t) * PAD
        pad = top + LEV
        ref[top:pad] = field(t)
        if t < 5:
            ref[pad : pad + 5] = slab[FULL + 5 * t : FULL + 5 * t + 5]
            ref[pad + 5 : pad + 6] = jnp.zeros((1, 128), F32)
        else:
            ref[pad : pad + 1] = kappa_ref[pl.ds(row, 1), :]
            ref[pad + 1 : pad + 6] = jnp.zeros((5, 128), F32)


def unpacked_matrix(slabs, slab):
    half = LEV // 2
    slab[...] = jnp.zeros_like(slab)
    for t in range(5):
        slab[FULL + 5 * t : FULL + 5 * t + 5] = slabs(t)[LEV : LEV + 5]
    both = slab[FULL : FULL + 32]
    low = lax.broadcasted_iota(jnp.int32, both.shape, 1) < LEV
    slab[0:half] = jnp.where(low, both, 0.0)[:half]
    slab[half:LEV] = jnp.where(low, pltpu.roll(both, 64, 1), 0.0)[:half]
    return slab[0:FULL]


def prepare_kernel(halo, *refs):
    sources, refs = refs[:10], refs[10:]
    feed_ref, sib_ref, cross_ref, *refs = refs
    local, (names, slab, arrived) = refs[:10], refs[10:]
    lists, (lam_ref, inv_ref, kappa_ref) = local[:4], local[4:7]
    child_ref, child_inv, child_kappa = local[7:10]
    rows, crows = kappa_ref.shape[0], child_kappa.shape[0]
    pairs = [p for k, p in enumerate(zip(sources, local)) if k != 7]
    pairs[7:7] = [
        (sources[7].at[:, first : first + 8, :], child_ref.at[k])
        for k, first in enumerate((0, crows - 8))
    ]
    copies = [pltpu.make_async_copy(*pair, arrived.at[k]) for k, pair in enumerate(pairs)]
    for copy in copies:
        copy.start()
    for copy in copies[:5]:
        copy.wait()
    cells, targets, weights, later = columns(names, lists)

    def level_rows(t, r):
        return lam_ref[pl.ds(t * LEV * rows + r, LEV, stride=rows), :]

    marks = [jnp.where(hits(cells, r), 1.0, 0.0).astype(BF16) for r in range(rows)]
    for g in range(3):
        total = jnp.zeros((cells.shape[0], MARK), F32)
        for r in range(rows):
            both = [padded_levels(level_rows(2 * g + t, r)) for t in range(2)]
            total = total + picked(jnp.concatenate(both, axis=0), marks[r])
        feed_ref[0, g] = feed_row(total, weights, targets, later)
    slab[...] = jnp.zeros_like(slab)
    even = on_even()
    for copy in copies[5:]:
        copy.wait()
    edge = child_ref.shape[1] * 8
    child_rows = child_ref.reshape(2 * edge, 128)
    for ref, head in ((sib_ref, ~even), (cross_ref, even)):
        r = jnp.where(head, 0, rows - 1)
        left = kept(cells, weights, r)
        field = lambda t: level_rows(t, r) * left
        pack_row(ref, halo, field, inv_ref, kappa_ref, r, rows, slab)
        for j in range(halo):
            r = jnp.where(head, j, crows - halo + j)
            top = jnp.where(head, j, edge + 8 - halo + j)
            field = lambda t: child_rows[pl.ds(t * LEV * 8 + top, LEV, stride=8), :]
            pack_row(ref, j, field, child_inv, child_kappa, r, crows, slab)


def prepare(lists, lam, inv, kappa, child, child_inv, child_kappa, halo):
    slots = lists[0].shape[1]
    edge = (halo + 1) * 6 * PAD
    operands = (*lists, lam, inv, kappa, child, child_inv, child_kappa)
    return pl.pallas_call(
        functools.partial(prepare_kernel, halo),
        in_specs=[pl.BlockSpec(memory_space=pltpu.HBM)] * len(operands),
        out_shape=(
            jax.ShapeDtypeStruct((1, 3, slots, 128), F32),
            jax.ShapeDtypeStruct((edge, 128), F32),
            jax.ShapeDtypeStruct((edge, 128), F32),
        ),
        scratch_shapes=[
            pltpu.VMEM((2, x.shape[0], 8, 128) if x is child else x.shape, x.dtype) for x in operands
        ]
        + [
            pltpu.VMEM((8, 128), F32),
            pltpu.VMEM((2 * FULL, 128), F32),
            pltpu.SemaphoreType.DMA((len(operands) + 1,)),
        ],
        compiler_params=pltpu.CompilerParams(vmem_limit_bytes=62 * 1024 * 1024),
        name="prepare",
    )(*operands)


def aligned(start, size):
    return pl.ds(start if isinstance(start, int) else pl.multiple_of(start, 8), size)


def feeds_of(group, feed_refs, places, slots):
    return jnp.concatenate(
        [
            ref[aligned(start + (3 * u + group) * slots, slots), :]
            for ref, (start, n) in zip(feed_refs, places)
            for u in range(n)
        ],
        axis=0,
    )


def edge_readers(first_edge, cross_ref, sib_ref):
    even = on_even()

    def edge_row(ref, j, t):
        return ref[aligned(((first_edge + j) * 6 + t) * PAD, PAD), :]

    def low_row(j, t):
        return jnp.where(even, edge_row(cross_ref, j, t), edge_row(sib_ref, j, t))

    def high_row(j, t):
        return jnp.where(even, edge_row(sib_ref, j, t), edge_row(cross_ref, j, t))

    return low_row, high_row


def set_up(rows, halo, lane, feeds, small, readers, onehot, chosen, edge_mats, coef, slab):
    grown = rows + 2 * halo
    total, slots = feeds.shape[0], small.shape[0] - rows
    cells, weights = small[0:slots, 0:1], small[0:slots, 2:3]
    low_row, high_row = readers
    kap = [None] * grown
    for j in range(halo):
        for q, row in ((j, low_row), (halo + rows + j, high_row)):
            slabs = functools.partial(row, j)
            edge_mats[q if q < halo else q - rows] = stacked_matrix(unpacked_matrix(slabs, slab))
            kap[q] = slabs(5)[LEV : LEV + 1, :]
    for r in range(rows):
        kap[halo + r] = small[slots + r : slots + r + 1, :]
    column = lax.broadcasted_iota(jnp.int32, (1, 128), 1)
    for q in range(grown):
        k = kap[q]
        coef[0, q : q + 1, :] = k
        coef[1, q : q + 1, :] = jnp.where(column == 0, 0.0, pltpu.roll(k, 1, 1))
        coef[2, q : q + 1, :] = jnp.where(column == 127, 0.0, pltpu.roll(k, 127, 1))
        coef[3, q : q + 1, :] = 1.0 - 4.0 * k
    for r in range(rows):
        coef[4, r : r + 1, :] = kept(cells, weights, r)

    base = ((lax.axis_index("tile") * rows - halo) * 128).astype(F32)
    where = jnp.transpose(feeds)[lane : lane + 1, :] - base
    inside = jnp.where((where >= 0.0) & (where < float(grown * 128)), 1.0, 0.0)
    earlier = lax.broadcasted_iota(jnp.int32, (total, total), 0) < lax.broadcasted_iota(
        jnp.int32, (total, total), 1
    )
    place = jnp.dot(
        jnp.broadcast_to(inside, (16, total)).astype(BF16),
        jnp.where(earlier, 1.0, 0.0).astype(BF16),
        preferred_element_type=F32,
    )[0:1]
    place = jnp.where(inside > 0.0, place, -1.0)
    rank = lax.broadcasted_iota(jnp.int32, (FEW, total), 0).astype(F32)
    chosen[...] = jnp.where(rank == place, 1.0, 0.0).astype(BF16)
    count = jnp.sum(inside).astype(jnp.int32)

    def mark(reached):
        for q in range(grown):
            onehot[q // 2, 0 : reached.shape[0], (q % 2) * 128 : (q % 2) * 128 + 128] = jnp.where(
                hits(reached, q), 1.0, 0.0
            ).astype(BF16)

    @pl.when(count <= FEW)
    def few():
        cell = jnp.where(lanes(total) == float(lane), feeds - base, 0.0)
        cell_hi, cell_lo = split(cell)
        reached = jnp.dot(chosen[...], cell_hi, preferred_element_type=F32)
        reached = reached + jnp.dot(chosen[...], cell_lo, preferred_element_type=F32)
        mark(reached[:, lane : lane + 1])

    @pl.when(count > FEW)
    def many():
        mark(feeds[:, lane : lane + 1] - base)

    return count


def steps_kernel(rows, halo, steps, gather, places, *refs):
    feed_refs, refs = refs[: len(places)], refs[len(places) :]
    (small_ref, lam_ref, cross_ref, sib_ref, mat_ref), refs = refs[:5], refs[5:]
    grown = rows + 2 * halo
    slots = small_ref.shape[0] - rows
    cells, targets, weights = (small_ref[0:slots, k : k + 1] for k in range(3))
    total = sum(n for _, n in places) * slots
    first_edge = 0 if gather else sib_ref.shape[0] // (6 * PAD) - 1
    low_row, high_row = edge_readers(first_edge, cross_ref, sib_ref)
    near_feeds = lambda group: feeds_of(group, feed_refs, places, slots)
    if gather:
        out_ref, given_ref, onehot, chosen, edge_mats, coef, slab, *refs = refs
        count = set_up(
            rows, halo, MARK, near_feeds(0), small_ref, (low_row, high_row), onehot, chosen, edge_mats, coef, slab
        )
    else:
        onehot, chosen, edge_mats, coef, count_ref, out_ref, *refs = refs
        given_ref = None
        count = jnp.max(count_ref[0:1, :]).astype(jnp.int32)
    held, sent, zbuf, *ybufs = refs

    def matrix(q):
        if halo <= q < halo + rows:
            return mat_ref[q - halo]
        return edge_mats[q if q < halo else q - rows]

    def start_few(group):
        feed_hi, feed_lo = split(near_feeds(group))
        near = jnp.dot(
            chosen[...], jnp.concatenate([feed_hi, feed_lo], axis=1), preferred_element_type=F32
        )
        near = [jnp.transpose(near[:, k : k + 128])[:MARK, :].astype(BF16) for k in (0, 128)]
        left = jnp.concatenate(near, axis=1)

        def arrive(pair):
            marks = onehot[pair, 0:FEW, :]
            return jnp.dot(left, jnp.concatenate([marks, marks], axis=0), preferred_element_type=F32)

        return arrive

    def start_many(group):
        turned = [jnp.transpose(x.astype(F32))[:MARK, :] for x in split(near_feeds(group))]
        left = jnp.concatenate(turned, axis=0).astype(BF16)

        def arrive(pair):
            both = jnp.dot(left, onehot[pair], preferred_element_type=F32)
            return both[:MARK] + both[MARK:]

        return arrive

    def copy_out(group):
        size = 2 * LEV * rows
        return pltpu.make_async_copy(
            held.at[group], out_ref.at[aligned(group * size, size), :], sent.at[group]
        )

    def finish(group, totals):
        if gather:
            given_ref[0, group] = feed_row(totals[0], weights, targets)
        copy_out(group).start()

    def plan_of(at, group, arrive):
        arrived, totals = {}, []
        tail_rows = jnp.zeros((FULL - PAD, 256), F32)

        def store(q, z):
            hi, lo = split(jnp.concatenate([z, tail_rows], axis=0))
            zbuf[at, q, 0:FULL] = hi
            zbuf[at, q, FULL : 2 * FULL] = lo

        def begin(q):
            if q % 2 == 0:
                arrived[q // 2] = arrive(q // 2)
            here = arrived[q // 2][:, (q % 2) * 128 : (q % 2) * 128 + 128]
            parts = []
            r = q - halo
            for t in range(2):
                tracer = 2 * group + t
                if 0 <= r < rows:
                    x = lam_ref[pl.ds(tracer * LEV * rows + r, LEV, stride=rows), :]
                    x = padded_levels(x)
                    if not gather:
                        x = x * coef[4, r : r + 1, :]
                else:
                    x = low_row(q, tracer) if q < halo else high_row(q - halo - rows, tracer)
                parts.append(x + here[t * PAD : (t + 1) * PAD])
            store(q, jnp.concatenate(parts, axis=1))

        def lift(k, q):
            z = zbuf[at, q]
            y = jnp.dot(
                matrix(q)[:, : 3 * FULL],
                jnp.concatenate([z, z[:FULL]], axis=0),
                preferred_element_type=F32,
            )
            ybufs[k][at, q] = y[:PAD]

        def spread(k, q):
            parts = []
            for t in range(2):
                s = slice(t * 128, t * 128 + 128)
                y = ybufs[k][at, q, :, s]
                z = y * coef[3, q : q + 1, :]
                z = z + pltpu.roll(y, 1, 1) * coef[1, q : q + 1, :]
                z = z + pltpu.roll(y, 127, 1) * coef[2, q : q + 1, :]
                z = z + ybufs[k][at, q - 1, :, s] * coef[0, q - 1 : q, :]
                z = z + ybufs[k][at, q + 1, :, s] * coef[0, q + 1 : q + 2, :]
                parts.append(z)
            if k < steps - 1:
                store(q, jnp.concatenate(parts, axis=1))
                return
            r = q - halo
            for t in range(2):
                z = parts[t]
                if gather:
                    z = z * coef[4, r : r + 1, :]
                held[group, pl.ds(t * LEV * rows + r, LEV, stride=rows), :] = z[:LEV]
            if gather:
                marks = jnp.where(hits(cells, r), 1.0, 0.0).astype(BF16)
                totals.append(picked(jnp.concatenate(parts, axis=0), marks))
                if len(totals) == 2:
                    totals[:] = [totals[0] + totals[1]]

        plan = []
        lag, wide, step = 5, 12, 12
        for q in range(grown):
            plan.append((q, 0, functools.partial(begin, q)))
            for k in range(steps):
                if k <= q < grown - k:
                    plan.append((q + lag + step * k, 1 + 2 * k, functools.partial(lift, k, q)))
                if k + 1 <= q < grown - k - 1:
                    plan.append((q + wide + step * k, 2 + 2 * k, functools.partial(spread, k, q)))
        plan.append((grown + step * steps + 1, 0, functools.partial(finish, group, totals)))
        return plan

    def run(start):
        if gather:

            def pair(group, _):
                for _, _, act in sorted(plan_of(0, group, start(group)), key=lambda p: p[:2]):
                    act()
                return 0

            lax.fori_loop(0, 3, pair, 0)
        else:
            plan = [p for g in range(3) for p in plan_of(g, g, start(g))]
            for _, _, act in sorted(plan, key=lambda p: p[:2]):
                act()

    @pl.when(count <= FEW)
    def few():
        run(start_few)

    @pl.when(count > FEW)
    def many():
        run(start_many)

    for group in range(3):
        copy_out(group).wait()


def set_up_shapes(rows, halo, total):
    grown = rows + 2 * halo
    return [
        ((grown // 2, total, 256), BF16),
        ((FEW, total), BF16),
        ((2 * halo, FULL, 256), BF16),
        ((5, (grown + 7) // 8 * 8, 128), F32),
    ]


def run_steps(small, feeds, lam, cross, sib, mats, halo, steps, ready=None):
    gather = ready is None
    rows = mats.shape[0]
    grown = rows + 2 * halo
    slots = small.shape[0] - rows
    places = tuple((start, n) for _, start, n in feeds)
    total = sum(n for _, n in places) * slots
    near = pl.BlockSpec(memory_space=pltpu.VMEM)
    out_shape = [jax.ShapeDtypeStruct(lam.shape, F32)]
    out_specs = [pl.BlockSpec(memory_space=pl.ANY)]
    scratch = []
    if gather:
        out_shape.append(jax.ShapeDtypeStruct((1, 3, slots, 128), F32))
        out_specs.append(near)
        scratch = [pltpu.VMEM(*x) for x in set_up_shapes(rows, halo, total)]
        scratch.append(pltpu.VMEM((2 * FULL, 128), F32))
    lots = 1 if gather else 3
    operands = [x for x, _, _ in feeds] + [small, lam, cross, sib, mats, *(ready or [])]
    return pl.pallas_call(
        functools.partial(steps_kernel, rows, halo, steps, gather, places),
        in_specs=[near] * len(operands),
        out_specs=out_specs,
        out_shape=out_shape,
        scratch_shapes=scratch
        + [
            pltpu.VMEM((3, 2 * LEV * rows, 128), F32),
            pltpu.SemaphoreType.DMA((3,)),
            pltpu.VMEM((lots, grown, 2 * FULL, 256), BF16),
        ]
        + [pltpu.VMEM((lots, grown, PAD, 256), F32) for _ in range(steps)],
        compiler_params=pltpu.CompilerParams(vmem_limit_bytes=VMEM_LIMIT),
        name="child" if gather else "parent",
    )(*operands)


def exchange(x, pairs):
    return lax.ppermute(x, "tile", [p for a, b in pairs for p in ((a, b), (b, a))])


def sibling(x):
    return exchange(x, [(i, i + 1) for i in range(0, lax.axis_size("tile"), 2)])


def beyond(x, chips):
    count = lax.axis_size("tile")
    first, distance = (1, 1) if chips == 1 else (0, 2 * chips + 1)
    return exchange(x, [(i, i + distance) for i in range(first, count - distance, 2)])


def rows_of(x):
    return x.reshape(-1, 128)


def per_device(
    lam_parent,
    lam_child,
    kappa_parent,
    kappa_child,
    inv_parent,
    inv_child,
    bnd_child,
    bnd_parent,
    bnd_weight,
    upd_parent,
    upd_child,
    upd_weight,
):
    upd = [x.reshape(1, -1) for x in (upd_parent, upd_child, upd_weight)]
    bnd = [x.reshape(1, -1) for x in (bnd_child, bnd_parent, bnd_weight)]
    flat_parent = lam_parent.reshape(-1, 128)
    flat_child = lam_child.reshape(-1, 128)
    inv_parent, inv_child = (
        jnp.transpose(x, (1, 0, 2)).reshape(-1, x.shape[2]) for x in (inv_parent, inv_child)
    )
    feed, to_sib, to_cross = prepare(
        [*upd, bnd[1]],
        flat_parent,
        inv_parent,
        kappa_parent,
        flat_child.reshape(-1, kappa_child.shape[0], 128),
        inv_child,
        kappa_child,
        3,
    )
    cross, sib = beyond(to_cross, 1), sibling(to_sib)

    def all_near(own, ready):
        beside = sibling(own)
        chip = jnp.concatenate([own, beside], axis=0)
        three, two, one = beyond(beside, 3), beyond(chip, 2), beyond(chip, 1)
        fetched = gathered(three, two, one, ready)
        return [(rows_of(chip), 0, 2), (rows_of(fetched), 0, 4), (rows_of(sibling(fetched)), 0, 5)]

    mats, field, small = stage(bnd, inv_child, kappa_child, flat_child)
    feeds = all_near(feed, mats)
    adj_child, given = run_steps(small, feeds, field, cross, sib, mats, 3, 3)
    mats, field, small, *ready = stage(upd, inv_parent, kappa_parent, flat_parent, 1, feeds, (cross, sib))
    feeds = all_near(given, mats)
    (adj_parent,) = run_steps(small, feeds, field, cross, sib, mats, 1, 1, ready)
    return adj_parent.reshape(lam_parent.shape), adj_child.reshape(lam_child.shape)


def solution(mesh):
    field, plane = P(None, None, "tile", None), P("tile", None)
    cube, line = P("tile", None, None), P("tile")
    in_specs = (field, field, plane, plane, cube, cube) + (line,) * 6
    return jax.shard_map(
        per_device, mesh=mesh, in_specs=in_specs, out_specs=(field, field), check_vma=False
    )
```

```python
import functools

import jax
import jax.numpy as jnp
from jax import lax
from jax.experimental import pallas as pl
from jax.experimental.pallas import tpu as pltpu
from jax.sharding import PartitionSpec as P

F32, BF16 = jnp.float32, jnp.bfloat16
LEV, PAD, FULL = 50, 56, 64
FEW = 128
MARK = 2 * PAD
VMEM_LIMIT = 32 * 1024 * 1024


def columns(rows, lists):
    rows[...] = jnp.zeros_like(rows)
    for k, ref in enumerate(lists):
        rows[k : k + 1, 0 : ref.shape[1]] = ref[...].astype(F32)
    turned = jnp.transpose(rows[...])[: lists[0].shape[1]]
    return [turned[:, k : k + 1] for k in range(len(lists))]


def on_even():
    return lax.rem(lax.axis_index("tile"), 2) == 0


def split(x):
    hi = x.astype(BF16)
    return hi, (x - hi.astype(F32)).astype(BF16)


def lanes(rows):
    return lax.broadcasted_iota(jnp.int32, (rows, 128), 1).astype(F32)


def hits(cells, row):
    return cells == lanes(cells.shape[0]) + jnp.asarray(row * 128, F32)


def kept(cells, weights, row):
    return 1.0 - jnp.sum(jnp.where(hits(cells, row), weights, 0.0), axis=0, keepdims=True)


def padded_levels(x):
    return jnp.concatenate([x, jnp.zeros((PAD - LEV, 128), F32)], axis=0)


def picked(fields, marks):
    hi, lo = split(fields)
    return lax.dot_general(
        jnp.concatenate([marks, marks], axis=1),
        jnp.concatenate([hi, lo], axis=1),
        (((1,), (1,)), ((), ())),
        preferred_element_type=F32,
    )


def feed_row(sums, weights, *targets):
    row = jnp.concatenate([sums * weights, jnp.zeros((sums.shape[0], 128 - MARK), F32)], axis=1)
    for k, target in enumerate(targets):
        row = jnp.where(lanes(sums.shape[0]) == float(MARK + k), target, row)
    return row


def stacked_matrix(slab):
    turned = jnp.transpose(slab)[:FULL, :]
    wide = jnp.concatenate([turned, jnp.zeros((FULL, 128 - FULL), F32)], axis=1)
    hi = wide.astype(BF16).astype(F32)
    lo = wide - hi
    return jnp.concatenate(
        [hi + pltpu.roll(hi, FULL, 1), lo + pltpu.roll(lo, FULL, 1)], axis=1
    ).astype(BF16)


def stage_kernel(rows, halo, places, *refs):
    lists, refs = refs[:3], refs[3:]
    (inv_ref, kappa_ref, lam_ref), refs = refs[:3], refs[3:]
    feed_refs, refs = refs[: len(places)], refs[len(places) :]
    if places:
        cross_ref, sib_ref, *refs = refs
    mats_ref, field_ref, small_ref, *refs = refs
    ready, (names, slab, arrived) = refs[:-3], refs[-3:]
    copy = pltpu.make_async_copy(lam_ref, field_ref, arrived)
    copy.start()
    slots = lists[0].shape[1]
    lane = lax.broadcasted_iota(jnp.int32, (slots, 128), 1)
    small = jnp.zeros((slots, 128), F32)
    for k, column in enumerate(columns(names, lists)):
        small = jnp.where(lane == k, column, small)
    small_ref[0:slots] = small
    small_ref[slots : slots + rows] = kappa_ref[...]
    slab[...] = jnp.zeros_like(slab)
    for r in range(rows):
        slab[0:LEV, 0:LEV] = inv_ref[pl.ds(r, LEV, stride=rows), :]
        mats_ref[r] = stacked_matrix(slab[0:FULL])
    if places:
        *ready, count_ref = ready
        readers = edge_readers(sib_ref.shape[0] // (6 * PAD) - halo, cross_ref, sib_ref)
        feeds = feeds_of(0, feed_refs, places, slots)
        count = set_up(rows, halo, MARK + 1, feeds, small_ref, readers, *ready, slab)
        count_ref[...] = jnp.zeros_like(count_ref) + count.astype(F32)
    copy.wait()


def stage(lists, inv, kappa, lam, halo=0, feeds=(), edges=()):
    rows = kappa.shape[0]
    slots = lists[0].shape[1]
    places = tuple((start, n) for _, start, n in feeds)
    near, shape = pl.BlockSpec(memory_space=pltpu.VMEM), jax.ShapeDtypeStruct
    extra = []
    if feeds:
        total = sum(n for _, n in places) * slots
        extra = [shape(*x) for x in set_up_shapes(rows, halo, total)] + [shape((8, 128), F32)]
    operands = [x for x, _, _ in feeds] + list(edges)
    return pl.pallas_call(
        functools.partial(stage_kernel, rows, halo, places),
        in_specs=[near] * 5 + [pl.BlockSpec(memory_space=pl.ANY)] + [near] * len(operands),
        out_shape=[
            shape((rows, FULL, 256), BF16),
            shape(lam.shape, F32),
            shape((slots + rows, 128), F32),
            *extra,
        ],
        scratch_shapes=[
            pltpu.VMEM((8, 128), F32),
            pltpu.VMEM((2 * FULL, 128), F32),
            pltpu.SemaphoreType.DMA(()),
        ],
        compiler_params=pltpu.CompilerParams(vmem_limit_bytes=VMEM_LIMIT),
        name="stage",
    )(*lists, inv, kappa, lam, *operands)


def gathered_kernel(count, *refs):
    parts, out_ref, start = refs[:count], refs[-1], 0
    for ref in parts:
        out_ref[start : start + ref.shape[0]] = ref[...]
        start += ref.shape[0]


def gathered(parts, ready):
    units = sum(x.shape[0] for x in parts)
    return pl.pallas_call(
        functools.partial(gathered_kernel, len(parts)),
        in_specs=[pl.BlockSpec(memory_space=pltpu.VMEM)] * len(parts) + [pl.BlockSpec(memory_space=pl.ANY)],
        out_shape=jax.ShapeDtypeStruct((units, *parts[0].shape[1:]), F32),
        compiler_params=pltpu.CompilerParams(vmem_limit_bytes=VMEM_LIMIT),
        name="gathered",
    )(*parts, ready)


def pack_row(ref, j, field, inv_ref, kappa_ref, row, rows, slab):
    slab[0:LEV, 0:LEV] = inv_ref[pl.ds(row, LEV, stride=rows), :]
    slab[FULL : FULL + 32] = slab[0:32] + pltpu.roll(slab[LEV // 2 : LEV // 2 + 32], 64, 1)
    for t in range(6):
        top = (6 * j + t) * PAD
        pad = top + LEV
        ref[top:pad] = field(t)
        if t < 5:
            ref[pad : pad + 5] = slab[FULL + 5 * t : FULL + 5 * t + 5]
            ref[pad + 5 : pad + 6] = jnp.zeros((1, 128), F32)
        else:
            ref[pad : pad + 1] = kappa_ref[pl.ds(row, 1), :]
            ref[pad + 1 : pad + 6] = jnp.zeros((5, 128), F32)


def unpacked_matrix(slabs, slab):
    half = LEV // 2
    slab[...] = jnp.zeros_like(slab)
    for t in range(5):
        slab[FULL + 5 * t : FULL + 5 * t + 5] = slabs(t)[LEV : LEV + 5]
    both = slab[FULL : FULL + 32]
    low = lax.broadcasted_iota(jnp.int32, both.shape, 1) < LEV
    slab[0:half] = jnp.where(low, both, 0.0)[:half]
    slab[half:LEV] = jnp.where(low, pltpu.roll(both, 64, 1), 0.0)[:half]
    return slab[0:FULL]


def prepare_kernel(halo, *refs):
    sources, refs = refs[:10], refs[10:]
    feed_ref, sib_ref, cross_ref, *refs = refs
    local, (names, slab, arrived) = refs[:10], refs[10:]
    lists, (lam_ref, inv_ref, kappa_ref) = local[:4], local[4:7]
    child_ref, child_inv, child_kappa = local[7:10]
    rows, crows = kappa_ref.shape[0], child_kappa.shape[0]
    pairs = [p for k, p in enumerate(zip(sources, local)) if k != 7]
    pairs[7:7] = [
        (sources[7].at[:, first : first + 8, :], child_ref.at[k])
        for k, first in enumerate((0, crows - 8))
    ]
    copies = [pltpu.make_async_copy(*pair, arrived.at[k]) for k, pair in enumerate(pairs)]
    for copy in copies:
        copy.start()
    for copy in copies[:5]:
        copy.wait()
    cells, targets, weights, later = columns(names, lists)

    def level_rows(t, r):
        return lam_ref[pl.ds(t * LEV * rows + r, LEV, stride=rows), :]

    marks = [jnp.where(hits(cells, r), 1.0, 0.0).astype(BF16) for r in range(rows)]
    for g in range(3):
        total = jnp.zeros((cells.shape[0], MARK), F32)
        for r in range(rows):
            both = [padded_levels(level_rows(2 * g + t, r)) for t in range(2)]
            total = total + picked(jnp.concatenate(both, axis=0), marks[r])
        feed_ref[0, g] = feed_row(total, weights, targets, later)
    slab[...] = jnp.zeros_like(slab)
    even = on_even()
    for copy in copies[5:]:
        copy.wait()
    edge = child_ref.shape[1] * 8
    child_rows = child_ref.reshape(2 * edge, 128)
    for ref, head in ((sib_ref, ~even), (cross_ref, even)):
        r = jnp.where(head, 0, rows - 1)
        left = kept(cells, weights, r)
        field = lambda t: level_rows(t, r) * left
        pack_row(ref, halo, field, inv_ref, kappa_ref, r, rows, slab)
        for j in range(halo):
            r = jnp.where(head, j, crows - halo + j)
            top = jnp.where(head, j, edge + 8 - halo + j)
            field = lambda t: child_rows[pl.ds(t * LEV * 8 + top, LEV, stride=8), :]
            pack_row(ref, j, field, child_inv, child_kappa, r, crows, slab)


def prepare(lists, lam, inv, kappa, child, child_inv, child_kappa, halo):
    slots = lists[0].shape[1]
    edge = (halo + 1) * 6 * PAD
    operands = (*lists, lam, inv, kappa, child, child_inv, child_kappa)
    return pl.pallas_call(
        functools.partial(prepare_kernel, halo),
        in_specs=[pl.BlockSpec(memory_space=pltpu.HBM)] * len(operands),
        out_shape=(
            jax.ShapeDtypeStruct((1, 3, slots, 128), F32),
            jax.ShapeDtypeStruct((edge, 128), F32),
            jax.ShapeDtypeStruct((edge, 128), F32),
        ),
        scratch_shapes=[
            pltpu.VMEM((2, x.shape[0], 8, 128) if x is child else x.shape, x.dtype) for x in operands
        ]
        + [
            pltpu.VMEM((8, 128), F32),
            pltpu.VMEM((2 * FULL, 128), F32),
            pltpu.SemaphoreType.DMA((len(operands) + 1,)),
        ],
        compiler_params=pltpu.CompilerParams(vmem_limit_bytes=62 * 1024 * 1024),
        name="prepare",
    )(*operands)


def aligned(start, size):
    return pl.ds(start if isinstance(start, int) else pl.multiple_of(start, 8), size)


def feeds_of(group, feed_refs, places, slots):
    return jnp.concatenate(
        [
            ref[aligned(start + (3 * u + group) * slots, slots), :]
            for ref, (start, n) in zip(feed_refs, places)
            for u in range(n)
        ],
        axis=0,
    )


def edge_readers(first_edge, cross_ref, sib_ref):
    even = on_even()

    def edge_row(ref, j, t):
        return ref[aligned(((first_edge + j) * 6 + t) * PAD, PAD), :]

    def low_row(j, t):
        return jnp.where(even, edge_row(cross_ref, j, t), edge_row(sib_ref, j, t))

    def high_row(j, t):
        return jnp.where(even, edge_row(sib_ref, j, t), edge_row(cross_ref, j, t))

    return low_row, high_row


def set_up(rows, halo, lane, feeds, small, readers, onehot, chosen, edge_mats, coef, slab):
    grown = rows + 2 * halo
    total, slots = feeds.shape[0], small.shape[0] - rows
    cells, weights = small[0:slots, 0:1], small[0:slots, 2:3]
    low_row, high_row = readers
    kap = [None] * grown
    for j in range(halo):
        for q, row in ((j, low_row), (halo + rows + j, high_row)):
            slabs = functools.partial(row, j)
            edge_mats[q if q < halo else q - rows] = stacked_matrix(unpacked_matrix(slabs, slab))
            kap[q] = slabs(5)[LEV : LEV + 1, :]
    for r in range(rows):
        kap[halo + r] = small[slots + r : slots + r + 1, :]
    column = lax.broadcasted_iota(jnp.int32, (1, 128), 1)
    for q in range(grown):
        k = kap[q]
        coef[0, q : q + 1, :] = k
        coef[1, q : q + 1, :] = jnp.where(column == 0, 0.0, pltpu.roll(k, 1, 1))
        coef[2, q : q + 1, :] = jnp.where(column == 127, 0.0, pltpu.roll(k, 127, 1))
        coef[3, q : q + 1, :] = 1.0 - 4.0 * k
    for r in range(rows):
        coef[4, r : r + 1, :] = kept(cells, weights, r)

    base = ((lax.axis_index("tile") * rows - halo) * 128).astype(F32)
    where = jnp.transpose(feeds)[lane : lane + 1, :] - base
    inside = jnp.where((where >= 0.0) & (where < float(grown * 128)), 1.0, 0.0)
    earlier = lax.broadcasted_iota(jnp.int32, (total, total), 0) < lax.broadcasted_iota(
        jnp.int32, (total, total), 1
    )
    place = jnp.dot(
        jnp.broadcast_to(inside, (16, total)).astype(BF16),
        jnp.where(earlier, 1.0, 0.0).astype(BF16),
        preferred_element_type=F32,
    )[0:1]
    place = jnp.where(inside > 0.0, place, -1.0)
    rank = lax.broadcasted_iota(jnp.int32, (FEW, total), 0).astype(F32)
    chosen[...] = jnp.where(rank == place, 1.0, 0.0).astype(BF16)
    count = jnp.sum(inside).astype(jnp.int32)

    def mark(reached):
        for q in range(grown):
            onehot[q // 2, 0 : reached.shape[0], (q % 2) * 128 : (q % 2) * 128 + 128] = jnp.where(
                hits(reached, q), 1.0, 0.0
            ).astype(BF16)

    @pl.when(count <= FEW)
    def few():
        cell = jnp.where(lanes(total) == float(lane), feeds - base, 0.0)
        cell_hi, cell_lo = split(cell)
        reached = jnp.dot(chosen[...], cell_hi, preferred_element_type=F32)
        reached = reached + jnp.dot(chosen[...], cell_lo, preferred_element_type=F32)
        mark(reached[:, lane : lane + 1])

    @pl.when(count > FEW)
    def many():
        mark(feeds[:, lane : lane + 1] - base)

    return count


def steps_kernel(rows, halo, steps, gather, places, *refs):
    feed_refs, refs = refs[: len(places)], refs[len(places) :]
    (small_ref, lam_ref, cross_ref, sib_ref, mat_ref), refs = refs[:5], refs[5:]
    grown = rows + 2 * halo
    slots = small_ref.shape[0] - rows
    cells, targets, weights = (small_ref[0:slots, k : k + 1] for k in range(3))
    total = sum(n for _, n in places) * slots
    first_edge = 0 if gather else sib_ref.shape[0] // (6 * PAD) - 1
    low_row, high_row = edge_readers(first_edge, cross_ref, sib_ref)
    near_feeds = lambda group: feeds_of(group, feed_refs, places, slots)
    if gather:
        out_ref, given_ref, onehot, chosen, edge_mats, coef, slab, *refs = refs
        count = set_up(
            rows, halo, MARK, near_feeds(0), small_ref, (low_row, high_row), onehot, chosen, edge_mats, coef, slab
        )
    else:
        onehot, chosen, edge_mats, coef, count_ref, out_ref, *refs = refs
        given_ref = None
        count = jnp.max(count_ref[0:1, :]).astype(jnp.int32)
    held, sent, zbuf, *ybufs = refs

    def matrix(q):
        if halo <= q < halo + rows:
            return mat_ref[q - halo]
        return edge_mats[q if q < halo else q - rows]

    def start_few(group):
        feed_hi, feed_lo = split(near_feeds(group))
        near = jnp.dot(
            chosen[...], jnp.concatenate([feed_hi, feed_lo], axis=1), preferred_element_type=F32
        )
        near = [jnp.transpose(near[:, k : k + 128])[:MARK, :].astype(BF16) for k in (0, 128)]
        left = jnp.concatenate(near, axis=1)

        def arrive(pair):
            marks = onehot[pair, 0:FEW, :]
            return jnp.dot(left, jnp.concatenate([marks, marks], axis=0), preferred_element_type=F32)

        return arrive

    def start_many(group):
        turned = [jnp.transpose(x.astype(F32))[:MARK, :] for x in split(near_feeds(group))]
        left = jnp.concatenate(turned, axis=0).astype(BF16)

        def arrive(pair):
            both = jnp.dot(left, onehot[pair], preferred_element_type=F32)
            return both[:MARK] + both[MARK:]

        return arrive

    def copy_out(group):
        size = 2 * LEV * rows
        return pltpu.make_async_copy(
            held.at[group], out_ref.at[aligned(group * size, size), :], sent.at[group]
        )

    def finish(group, totals):
        if gather:
            given_ref[0, group] = feed_row(totals[0], weights, targets)
        copy_out(group).start()

    def plan_of(at, group, arrive):
        arrived, totals = {}, []
        tail_rows = jnp.zeros((FULL - PAD, 256), F32)

        def store(q, z):
            hi, lo = split(jnp.concatenate([z, tail_rows], axis=0))
            zbuf[at, q, 0:FULL] = hi
            zbuf[at, q, FULL : 2 * FULL] = lo

        def begin(q):
            if q % 2 == 0:
                arrived[q // 2] = arrive(q // 2)
            here = arrived[q // 2][:, (q % 2) * 128 : (q % 2) * 128 + 128]
            parts = []
            r = q - halo
            for t in range(2):
                tracer = 2 * group + t
                if 0 <= r < rows:
                    x = lam_ref[pl.ds(tracer * LEV * rows + r, LEV, stride=rows), :]
                    x = padded_levels(x)
                    if not gather:
                        x = x * coef[4, r : r + 1, :]
                else:
                    x = low_row(q, tracer) if q < halo else high_row(q - halo - rows, tracer)
                parts.append(x + here[t * PAD : (t + 1) * PAD])
            store(q, jnp.concatenate(parts, axis=1))

        def lift(k, q):
            z = zbuf[at, q]
            y = jnp.dot(
                matrix(q)[:, : 3 * FULL],
                jnp.concatenate([z, z[:FULL]], axis=0),
                preferred_element_type=F32,
            )
            ybufs[k][at, q] = y[:PAD]

        def spread(k, q):
            parts = []
            for t in range(2):
                s = slice(t * 128, t * 128 + 128)
                y = ybufs[k][at, q, :, s]
                z = y * coef[3, q : q + 1, :]
                z = z + pltpu.roll(y, 1, 1) * coef[1, q : q + 1, :]
                z = z + pltpu.roll(y, 127, 1) * coef[2, q : q + 1, :]
                z = z + ybufs[k][at, q - 1, :, s] * coef[0, q - 1 : q, :]
                z = z + ybufs[k][at, q + 1, :, s] * coef[0, q + 1 : q + 2, :]
                parts.append(z)
            if k < steps - 1:
                store(q, jnp.concatenate(parts, axis=1))
                return
            r = q - halo
            for t in range(2):
                z = parts[t]
                if gather:
                    z = z * coef[4, r : r + 1, :]
                held[group, pl.ds(t * LEV * rows + r, LEV, stride=rows), :] = z[:LEV]
            if gather:
                marks = jnp.where(hits(cells, r), 1.0, 0.0).astype(BF16)
                totals.append(picked(jnp.concatenate(parts, axis=0), marks))
                if len(totals) == 2:
                    totals[:] = [totals[0] + totals[1]]

        plan = []
        lag, wide, step = 5, 12, 12
        for q in range(grown):
            plan.append((q, 0, functools.partial(begin, q)))
            for k in range(steps):
                if k <= q < grown - k:
                    plan.append((q + lag + step * k, 1 + 2 * k, functools.partial(lift, k, q)))
                if k + 1 <= q < grown - k - 1:
                    plan.append((q + wide + step * k, 2 + 2 * k, functools.partial(spread, k, q)))
        plan.append((grown + step * steps + 1, 0, functools.partial(finish, group, totals)))
        return plan

    def run(start):
        if gather:

            def pair(group, _):
                for _, _, act in sorted(plan_of(0, group, start(group)), key=lambda p: p[:2]):
                    act()
                return 0

            lax.fori_loop(0, 3, pair, 0)
        else:
            plan = [p for g in range(3) for p in plan_of(g, g, start(g))]
            for _, _, act in sorted(plan, key=lambda p: p[:2]):
                act()

    @pl.when(count <= FEW)
    def few():
        run(start_few)

    @pl.when(count > FEW)
    def many():
        run(start_many)

    for group in range(3):
        copy_out(group).wait()


def set_up_shapes(rows, halo, total):
    grown = rows + 2 * halo
    return [
        ((grown // 2, total, 256), BF16),
        ((FEW, total), BF16),
        ((2 * halo, FULL, 256), BF16),
        ((5, (grown + 7) // 8 * 8, 128), F32),
    ]


def run_steps(small, feeds, lam, cross, sib, mats, halo, steps, ready=None):
    gather = ready is None
    rows = mats.shape[0]
    grown = rows + 2 * halo
    slots = small.shape[0] - rows
    places = tuple((start, n) for _, start, n in feeds)
    total = sum(n for _, n in places) * slots
    near = pl.BlockSpec(memory_space=pltpu.VMEM)
    out_shape = [jax.ShapeDtypeStruct(lam.shape, F32)]
    out_specs = [pl.BlockSpec(memory_space=pl.ANY)]
    scratch = []
    if gather:
        out_shape.append(jax.ShapeDtypeStruct((1, 3, slots, 128), F32))
        out_specs.append(near)
        scratch = [pltpu.VMEM(*x) for x in set_up_shapes(rows, halo, total)]
        scratch.append(pltpu.VMEM((2 * FULL, 128), F32))
    lots = 1 if gather else 3
    operands = [x for x, _, _ in feeds] + [small, lam, cross, sib, mats, *(ready or [])]
    return pl.pallas_call(
        functools.partial(steps_kernel, rows, halo, steps, gather, places),
        in_specs=[near] * len(operands),
        out_specs=out_specs,
        out_shape=out_shape,
        scratch_shapes=scratch
        + [
            pltpu.VMEM((3, 2 * LEV * rows, 128), F32),
            pltpu.SemaphoreType.DMA((3,)),
            pltpu.VMEM((lots, grown, 2 * FULL, 256), BF16),
        ]
        + [pltpu.VMEM((lots, grown, PAD, 256), F32) for _ in range(steps)],
        compiler_params=pltpu.CompilerParams(vmem_limit_bytes=VMEM_LIMIT),
        name="child" if gather else "parent",
    )(*operands)


def exchange(x, pairs):
    return lax.ppermute(x, "tile", [p for a, b in pairs for p in ((a, b), (b, a))])


def sibling(x):
    return exchange(x, [(i, i + 1) for i in range(0, lax.axis_size("tile"), 2)])


def beyond(x, chips):
    count = lax.axis_size("tile")
    first, distance = (1, 1) if chips == 1 else (0, 2 * chips + 1)
    return exchange(x, [(i, i + distance) for i in range(first, count - distance, 2)])


def rows_of(x):
    return x.reshape(-1, 128)


def per_device(
    lam_parent,
    lam_child,
    kappa_parent,
    kappa_child,
    inv_parent,
    inv_child,
    bnd_child,
    bnd_parent,
    bnd_weight,
    upd_parent,
    upd_child,
    upd_weight,
):
    upd = [x.reshape(1, -1) for x in (upd_parent, upd_child, upd_weight)]
    bnd = [x.reshape(1, -1) for x in (bnd_child, bnd_parent, bnd_weight)]
    flat_parent = lam_parent.reshape(-1, 128)
    flat_child = lam_child.reshape(-1, 128)
    inv_parent, inv_child = (
        jnp.transpose(x, (1, 0, 2)).reshape(-1, x.shape[2]) for x in (inv_parent, inv_child)
    )
    feed, to_sib, to_cross = prepare(
        [*upd, bnd[1]],
        flat_parent,
        inv_parent,
        kappa_parent,
        flat_child.reshape(-1, kappa_child.shape[0], 128),
        inv_child,
        kappa_child,
        3,
    )
    cross, sib = beyond(to_cross, 1), sibling(to_sib)

    def all_near(own, ready, relay):
        beside = sibling(own)
        chip = jnp.concatenate([own, beside], axis=0)
        one = beyond(chip, 1)
        if relay:
            parts = [one, beyond(jnp.concatenate([chip, one[:1]], axis=0), 2)]
        else:
            parts = [one, beyond(chip, 2), beyond(beside, 3)]
        fetched = gathered(parts, ready)
        return [(rows_of(chip), 0, 2), (rows_of(fetched), 0, 4), (rows_of(sibling(fetched)), 0, 5)]

    mats, field, small = stage(bnd, inv_child, kappa_child, flat_child)
    feeds = all_near(feed, mats, False)
    adj_child, given = run_steps(small, feeds, field, cross, sib, mats, 3, 3)
    mats, field, small, *ready = stage(upd, inv_parent, kappa_parent, flat_parent, 1, feeds, (cross, sib))
    feeds = all_near(given, mats, True)
    (adj_parent,) = run_steps(small, feeds, field, cross, sib, mats, 1, 1, ready)
    return adj_parent.reshape(lam_parent.shape), adj_child.reshape(lam_child.shape)


def solution(mesh):
    field, plane = P(None, None, "tile", None), P("tile", None)
    cube, line = P("tile", None, None), P("tile")
    in_specs = (field, field, plane, plane, cube, cube) + (line,) * 6
    return jax.shard_map(
        per_device, mesh=mesh, in_specs=in_specs, out_specs=(field, field), check_vma=False
    )
```
